256 devices in a mesh: band: 16 (over y, x_lo, core), blk: 16 (over z, x_hi).
Axes of the slice: x: 4 (x_hi: 2, x_lo: 2; x = x_hi * 2 + x_lo), y: 4, z: 8, core: 2. Of those that a mesh axis runs over, the one named last changes fastest.
Arguments:
- load_columns: float32 [16, 16, 4, 32, 384], P('band', 'blk'), may hold values from -6 to 6
- stiffness: float32 [16, 16, 4, 384, 384], P('band', 'blk')
- rigid_modes: bfloat16 [16, 16, 4, 36, 384], P('band', 'blk'), may hold values from -0.3125 to 0.3125
- neighbours: int32 [16, 16, 4, 8], P('band', 'blk'), may hold values from 0 to 5, as said below
- slot_valid: int32 [16, 16, 4, 8], P('band', 'blk'), may hold values from 0 to 1, as said below
- pair_left: int32 [16, 16, 4, 128], P('band', 'blk'), may hold values from 0 to 63
- pair_right: int32 [16, 16, 4, 128], P('band', 'blk'), may hold values from 0 to 63
- penalty: float32 [16, 16, 4, 128], P('band', 'blk'), may hold values from 0.1 to 1
Outputs:
- displacement: float32 [16, 16, 4, 32, 384], P('band', 'blk')
- residual: float32 [16, 16, 4, 32, 384], P('band', 'blk')
The draws below stay inside these ranges and needn't reach their ends.
Inputs may be any that keep to these rules, and one draw needn't show every extreme that they name: `neighbours`: only aggregates 2 * 1 to 2 of a device name entries from 4 to 4 + 1 - 1 (the next sector's device), only aggregates 3 * 1 to 3 name entries from 5 up (the next band's device), and no aggregate of the last band does; all other entries are below 4. `slot_valid`: the valid slots of each aggregate are a prefix of its slots, slot 0 always valid; some aggregate has all 8 slots valid.
All inputs are finite; a program needn't handle non-finite values.
Results may differ from the reference program's by a relative error of at most 0.0003.
Values sent between devices are 32-bit elements; how exact they have to be, the bound alone decides.
No kernel may reach another device: no remote copies, remote signals or barrier semaphores. Data moves between devices by JAX's collectives and lax.ppermute only.
A program may use at most 192 MiB of HBM per device.

```python
import math
import jax
import jax.numpy as jnp
from jax import lax

COLS = 32
BLOCKS = 64
DOF = 384
MODES = 36
SLOTS = 8
PAIRS_SLOT = 16
PAIRS = 128
AGG_DEV = 4
RIM = 1
PRE = 2
POST = 1
COARSE_SWEEPS = 4
CYCLES = 1
BANDS = 16
SECTORS = 16


def link_tables(key):
    extent = (BANDS, SECTORS, AGG_DEV, SLOTS)
    pick_key, cross_key, rim_key, degree_key = jax.random.split(jax.random.fold_in(key, 5), 4)
    local_pick = jax.random.randint(pick_key, extent, 0, AGG_DEV)
    crossing = jax.random.randint(cross_key, extent, 0, 2)
    rim_pick = jax.random.randint(rim_key, extent, 0, RIM)
    band_index = lax.broadcasted_iota(jnp.int32, extent, 0)
    aggregate_index = lax.broadcasted_iota(jnp.int32, extent, 2)
    facing_sector = (aggregate_index >= 2 * RIM) & (aggregate_index < 3 * RIM)
    facing_band = (aggregate_index >= 3 * RIM) & (aggregate_index < 4 * RIM) & (band_index < BANDS - 1)
    to_sector = facing_sector & (crossing == 1)
    to_band = facing_band & (crossing == 1)
    linked = jnp.where(to_sector, AGG_DEV + rim_pick, jnp.where(to_band, AGG_DEV + RIM + rim_pick, local_pick))
    linked = linked.at[0, 0, 3 * RIM, 0].set(AGG_DEV + 2 * RIM - 1).at[0, 0, 0, 0].set(0)
    degree = jax.random.randint(degree_key, extent[:3], 1, SLOTS + 1)
    degree = degree.at[0, 0, 0].set(SLOTS)
    slot_index = lax.broadcasted_iota(jnp.int32, extent, 3)
    valid_slots = (slot_index < degree[..., None]).astype(jnp.int32)
    return (linked.astype(jnp.int32), valid_slots)


def draw_neighbours(key, part):
    return link_tables(key)[0]


def draw_slot_valid(key, part):
    return link_tables(key)[1]


def draw_stiffness(key, part):
    extent = (BANDS, SECTORS, AGG_DEV, DOF, DOF)
    noise_key, scale_key = jax.random.split(jax.random.fold_in(key, 11))
    random_part = jax.random.normal(noise_key, extent, jnp.float32) * 0.06
    symmetric = (random_part + jnp.swapaxes(random_part, -1, -2)) * 0.70710678
    diagonal = 4.0 + 2.0 * jax.random.uniform(scale_key, extent[:-1], jnp.float32)
    identity = jnp.eye(DOF, dtype=jnp.float32)
    return (symmetric * (1.0 - identity) + identity * diagonal[..., None]).astype(jnp.float32)


def plant(values, rng, least, largest):
    longest = values.shape.index(max(values.shape))
    spots = []
    for shift in (0, 1):
        where = [jax.random.randint(jax.random.fold_in(rng, axis), (), 0, length) for axis, length in enumerate(values.shape)]
        where[longest] = (where[longest] + shift) % values.shape[longest]
        spots.append(tuple(where))
    return values.at[spots[0]].set(least).at[spots[1]].set(largest)


def shard_levels(own_key, shape, cuts, least, high):
    gain = 1.0
    for position, shards_of in cuts:
        draws = jax.random.uniform(jax.random.fold_in(jax.random.fold_in(own_key, 6), position), (shards_of,), jnp.float32, least / len(cuts), high / len(cuts))
        gain = gain * jnp.repeat(jnp.exp(draws), shape[position] // shards_of).reshape((-1,) + (1,) * (len(shape) - 1 - position))
    return gain


def centred(own_key, shape, width, bound, cuts=(), kind=jnp.bfloat16):
    entries = jax.random.normal(own_key, shape, jnp.float32) * width
    if len(cuts) > 0:
        entries = shard_levels(own_key, shape, cuts, -0.22, 0.18) * entries
    return jnp.clip(entries, min=-bound, max=bound).astype(kind)


def setup_inputs(seed: int = 0) -> dict:
    keys = jax.random.split(jax.random.key(seed), 9)
    return {
        "load_columns": centred(keys[0], (BANDS, SECTORS, AGG_DEV, COLS, DOF), 1.0, 6.0, ((0, 16), (1, 16)), jnp.float32),
        "stiffness": draw_stiffness(jax.random.fold_in(keys[8], 71), 0),
        "rigid_modes": centred(keys[2], (BANDS, SECTORS, AGG_DEV, MODES, DOF), DOF ** -0.5, 0.3125, ((0, 16), (1, 16))),
        "neighbours": draw_neighbours(jax.random.fold_in(keys[8], 71), 0),
        "slot_valid": draw_slot_valid(jax.random.fold_in(keys[8], 71), 0),
        "pair_left": plant(jax.random.randint(keys[5], (BANDS, SECTORS, AGG_DEV, PAIRS), 0, BLOCKS), jax.random.fold_in(keys[5], 1), 0, BLOCKS - 1).astype(jnp.int32),
        "pair_right": plant(jax.random.randint(keys[6], (BANDS, SECTORS, AGG_DEV, PAIRS), 0, BLOCKS), jax.random.fold_in(keys[6], 1), 0, BLOCKS - 1).astype(jnp.int32),
        "penalty": jnp.clip(jnp.exp(math.log(1.0) - 2.3025851 * jax.random.uniform(keys[7], (BANDS, SECTORS, AGG_DEV, PAIRS), jnp.float32) ** shard_levels(keys[7], (BANDS, SECTORS, AGG_DEV, PAIRS), ((0, 16), (1, 16)), -0.2, 0.2)), 0.1, 1.0),
    }


fine_damping = 0.6
coarse_damping = 0.7
highest = lax.Precision.HIGHEST

def block_rows(source):
    amount = source.shape[0]
    breadth = source.shape[1]
    return source.reshape(amount, breadth, BLOCKS, 6).transpose(0, 2, 1, 3).reshape(amount * BLOCKS, breadth * 6)

def unblock(summed, amount):
    breadth = summed.shape[1] // 6
    return summed.reshape(amount, BLOCKS, breadth, 6).transpose(0, 2, 1, 3).reshape(amount, breadth, BLOCKS * 6)

def pair_springs(source, near_rows, far_rows, weight):
    amount = source.shape[0]
    rows_all = block_rows(source)
    forces = weight[:, None] * (rows_all[near_rows] - rows_all[far_rows])
    summed = jax.ops.segment_sum(jnp.concatenate([forces, -forces]), jnp.concatenate([near_rows, far_rows]), num_segments=amount * BLOCKS)
    return unblock(summed, amount)

def pair_layout(neighbours, slot_valid, pair_left, pair_right, penalty):
    aggregates = neighbours.shape[0]
    target = jnp.repeat(neighbours, PAIRS_SLOT, axis=1)
    weight = penalty * jnp.repeat(slot_valid, PAIRS_SLOT, axis=1).astype(penalty.dtype)
    near_rows = (jnp.arange(aggregates, dtype=jnp.int32)[:, None] * BLOCKS + pair_left).reshape(-1).astype(jnp.int32)
    far_rows = (target * BLOCKS + pair_right).reshape(-1).astype(jnp.int32)
    return (target, weight, near_rows, far_rows)

def block_totals(near_rows, far_rows, weight):
    summed = jax.ops.segment_sum(jnp.concatenate([weight, weight]), jnp.concatenate([near_rows, far_rows]), num_segments=(AGG_DEV + 2 * RIM) * BLOCKS)
    return summed.reshape(AGG_DEV + 2 * RIM, BLOCKS)

def coarse_setup(packed):
    modes_here, sector_modes, band_modes, stiffness_here, near_here, far_here, weight_here, neighbours_here = packed
    modes_wide = modes_here.astype(jnp.float32)
    mode_rows = block_rows(jnp.concatenate([modes_wide, sector_modes, band_modes]))
    grouped = (AGG_DEV, SLOTS, PAIRS_SLOT, MODES, 6)
    near_modes = mode_rows[near_here].reshape(grouped)
    far_modes = mode_rows[far_here].reshape(grouped)
    scales = weight_here.reshape(AGG_DEV, SLOTS, PAIRS_SLOT, 1, 1)
    coupling = -jnp.einsum('aspkd,aspld->askl', scales * near_modes, far_modes, precision=highest)
    self_term = jnp.einsum('aspkd,aspld->akl', scales * near_modes, near_modes, precision=highest)
    other_term = jnp.einsum('aspkd,aspld->askl', scales * far_modes, far_modes, precision=highest)
    landed = jax.ops.segment_sum(other_term.reshape(AGG_DEV * SLOTS, MODES, MODES), neighbours_here.reshape(-1), num_segments=AGG_DEV + 2 * RIM)
    projected = jnp.einsum('akf,afg->akg', modes_wide, stiffness_here, precision=highest)
    galerkin = jnp.einsum('akg,alg->akl', projected, modes_wide, precision=highest)
    return (coupling, galerkin + self_term + landed[:AGG_DEV], landed[AGG_DEV:AGG_DEV + RIM], landed[AGG_DEV + RIM:])

def coarse_apply(coarse, rim_sector, rim_band, coupling, coarse_diagonal, neighbours_here):
    source = jnp.concatenate([coarse, rim_sector, rim_band])
    nearby = source[neighbours_here]
    result = jnp.einsum('akl,acl->ack', coarse_diagonal, coarse, precision=highest)
    result = result + jnp.einsum('askl,ascl->ack', coupling, nearby, precision=highest)
    reverse = jnp.einsum('askl,ack->ascl', coupling, coarse, precision=highest)
    landed = jax.ops.segment_sum(reverse.reshape(AGG_DEV * SLOTS, COLS, MODES), neighbours_here.reshape(-1), num_segments=AGG_DEV + 2 * RIM)
    return (result + landed[:AGG_DEV], landed[AGG_DEV:AGG_DEV + RIM], landed[AGG_DEV + RIM:])

def invert_block(block):
    triangle = jnp.linalg.cholesky(block)
    return jax.scipy.linalg.cho_solve((triangle, True), jnp.eye(block.shape[0], dtype=block.dtype))

def fine_device(packed):
    field_here, sector_here, band_here, stiffness_here, near_here, far_here, weight_here = packed
    source = jnp.concatenate([field_here, sector_here, band_here])
    springs = pair_springs(source, near_here, far_here, weight_here)
    bending = jnp.einsum('acf,afg->acg', field_here, stiffness_here, precision=highest)
    return (bending + springs[:AGG_DEV], springs[AGG_DEV:AGG_DEV + RIM], springs[AGG_DEV + RIM:])

def reference(load_columns, stiffness, rigid_modes, neighbours, slot_valid, pair_left, pair_right, penalty):
    devices = BANDS * SECTORS

    def flatten(values):
        return values.reshape((devices,) + values.shape[2:])

    def restore(values):
        return values.reshape((BANDS, SECTORS) + values.shape[1:])

    def ahead_all(values):
        sector_rim = jnp.roll(values[:, :, :RIM], -1, axis=1)
        upper_rows = values[1:, :, RIM:2 * RIM]
        band_rim = jnp.concatenate([upper_rows, jnp.zeros_like(values[:1, :, RIM:2 * RIM])], axis=0)
        return (sector_rim, band_rim)

    def behind_all(sector_part, band_part):
        return (jnp.roll(sector_part, 1, axis=1), jnp.concatenate([jnp.zeros_like(band_part[:1]), band_part[:-1]], axis=0))

    def add_all(values, sector_part, band_part):
        return values.at[:, :, :RIM].add(sector_part).at[:, :, RIM:2 * RIM].add(band_part)
    target, weight, near_rows, far_rows = jax.vmap(pair_layout)(flatten(neighbours), flatten(slot_valid), flatten(pair_left), flatten(pair_right), flatten(penalty))
    flat_weight = weight.reshape(devices, -1)
    totals = restore(jax.vmap(block_totals)(near_rows, far_rows, flat_weight))
    sector_part, band_part = behind_all(totals[:, :, AGG_DEV:AGG_DEV + RIM], totals[:, :, AGG_DEV + RIM:])
    totals = add_all(totals[:, :, :AGG_DEV], sector_part, band_part)
    fine_diagonal = jnp.diagonal(stiffness, axis1=3, axis2=4) + jnp.repeat(totals, 6, axis=3)
    reciprocal = 1.0 / fine_diagonal
    modes_wide = rigid_modes.astype(jnp.float32)
    sector_modes, band_modes = ahead_all(modes_wide)
    coupling, diagonal_own, sector_part, band_part = lax.map(coarse_setup, (flatten(rigid_modes), flatten(sector_modes), flatten(band_modes), flatten(stiffness), near_rows, far_rows, weight, flatten(neighbours)))
    sector_part, band_part = behind_all(restore(sector_part), restore(band_part))
    coarse_diagonal = add_all(restore(diagonal_own), sector_part, band_part)
    coarse_inverse = jax.vmap(invert_block)(coarse_diagonal.reshape(-1, MODES, MODES)).reshape(coarse_diagonal.shape)

    def fine_product(field):
        rim_sector, rim_band = ahead_all(field)
        own, sector_out, band_out = lax.map(fine_device, (flatten(field), flatten(rim_sector), flatten(rim_band), flatten(stiffness), near_rows, far_rows, flat_weight))
        sector_in, band_in = behind_all(restore(sector_out), restore(band_out))
        return add_all(restore(own), sector_in, band_in)

    def coarse_product(coarse):
        rim_sector, rim_band = ahead_all(coarse)
        own, sector_out, band_out = jax.vmap(coarse_apply)(flatten(coarse), flatten(rim_sector), flatten(rim_band), coupling, flatten(coarse_diagonal), flatten(neighbours))
        sector_in, band_in = behind_all(restore(sector_out), restore(band_out))
        return add_all(restore(own), sector_in, band_in)

    def coarse_solve(restricted):
        correction = coarse_damping * jnp.einsum('bsakl,bsacl->bsack', coarse_inverse, restricted, precision=highest)
        for sweep_index in range(1, COARSE_SWEEPS):
            misfit = restricted - coarse_product(correction)
            correction = correction + coarse_damping * jnp.einsum('bsakl,bsacl->bsack', coarse_inverse, misfit, precision=highest)
        return correction
    field = jnp.zeros_like(load_columns)
    residual = load_columns
    for cycle_index in range(CYCLES):
        for sweep_index in range(PRE):
            field = field + fine_damping * reciprocal[:, :, :, None, :] * residual
            residual = load_columns - fine_product(field)
        restricted = jnp.einsum('bsacf,bsakf->bsack', residual, modes_wide, precision=highest)
        field = field + jnp.einsum('bsack,bsakf->bsacf', coarse_solve(restricted), modes_wide, precision=highest)
        residual = load_columns - fine_product(field)
        for sweep_index in range(POST):
            field = field + fine_damping * reciprocal[:, :, :, None, :] * residual
            residual = load_columns - fine_product(field)
    return (field, residual)
```

```python
import jax
import jax.numpy as jnp
from jax import lax
from jax.experimental import pallas as pl
from jax.experimental.pallas import tpu as pltpu
from jax.sharding import PartitionSpec as P

COLS = 32
BLOCKS = 64
DOF = 384
MODES = 36
SLOTS = 8
PAIRS = 128
AGG = 4
LANES = 128
PAIRED = 3
MROWS = 40

fine_damping = 0.6
coarse_damping = 0.7
f32 = jnp.float32
bf16 = jnp.bfloat16

NN = (((1,), (0,)), ((), ()))
NT = (((1,), (1,)), ((), ()))


def dot(a, b, dims=NN):
    return lax.dot_general(a, b, dims, preferred_element_type=f32)


def exact(a, b, dims=NN):
    return lax.dot_general(
        a, b, dims, precision=lax.Precision.HIGHEST, preferred_element_type=f32
    )


def split2(x):
    hi = x.astype(bf16)
    lo = (x - hi.astype(f32)).astype(bf16)
    return hi, lo


def split3(x):
    hi = x.astype(bf16)
    rest = x - hi.astype(f32)
    mid = rest.astype(bf16)
    lo = (rest - mid.astype(f32)).astype(bf16)
    return hi, mid, lo


def mm3(x, whi, wlo, dims=NN):
    rows = x.shape[0]
    hi, lo = split2(x)
    first = dot(jnp.concatenate([hi, lo], axis=0), whi, dims)
    return first[:rows] + first[rows:] + dot(hi, wlo, dims)


def mm2(x, w, dims=NN):
    rows = x.shape[0]
    hi, lo = split2(x)
    both = dot(jnp.concatenate([hi, lo], axis=0), w, dims)
    return both[:rows] + both[rows:]


def mm_exact(x, w, dims=NN):
    rows = x.shape[0]
    parts = dot(jnp.concatenate(split3(x), axis=0), w, dims)
    return parts[:rows] + parts[rows : 2 * rows] + parts[2 * rows :]


def iota(shape, axis):
    return lax.broadcasted_iota(jnp.int32, shape, axis)


def permutation():
    i = iota((DOF, DOF), 0)
    j = iota((DOF, DOF), 1)
    return (i == 6 * (j & 63) + (j >> 6)).astype(f32).astype(bf16)


def permutation_back():
    i = iota((DOF, DOF), 0)
    j = iota((DOF, DOF), 1)
    return (j == 6 * (i & 63) + (i >> 6)).astype(f32).astype(bf16)


def hot_twice(index):
    k = iota((LANES, PAIRS), 0) & 63
    return (k == index.astype(jnp.int32)).astype(f32).astype(bf16)


def hot_paired(index):
    r = iota((LANES, 2 * PAIRS), 0)
    doubled = jnp.concatenate([index.astype(jnp.int32)] * 2, axis=1)
    want = doubled + 64 * (iota((1, 2 * PAIRS), 1) >> 7)
    return (r == want).astype(f32).astype(bf16)


def wide(t):
    return jnp.concatenate([t] * PAIRED, axis=1)


def stack_fields(v):
    rows = []
    for m in range(PAIRED):
        rows.append(jnp.concatenate([x[:, m * LANES : (m + 1) * LANES] for x in v], axis=1))
    return jnp.concatenate(rows, axis=0)


def unstack_fields(y, count):
    out = []
    for a in range(count):
        parts = [
            y[m * COLS : (m + 1) * COLS, a * LANES : (a + 1) * LANES] for m in range(PAIRED)
        ]
        out.append(jnp.concatenate(parts, axis=1))
    return out


def rows_of(x):
    return jnp.concatenate([x[:, m * LANES : (m + 1) * LANES] for m in range(PAIRED)], axis=0)


def lanes_of(x):
    r = x.shape[0] // PAIRED
    return jnp.concatenate([x[m * r : (m + 1) * r] for m in range(PAIRED)], axis=1)


def local_product(v, khi, klo, ghi, glo, cross):
    springs = unstack_fields(mm3(stack_fields(v), ghi, glo), AGG)
    return [
        mm3(v[a], khi[a], klo[a]) + (springs[a] + v[a] * cross[a]) for a in range(AGG)
    ]


def to_own(vh, xhi, xlo):
    return lanes_of(mm3(rows_of(vh), xhi, xlo, NT))


def to_halo(v, xhi, xlo):
    return lanes_of(mm3(rows_of(v), xhi, xlo))


def pick(flag, a, b):
    return jnp.where(flag, a, b)


def send(parity, message, blk1, blk0, band1, band0):
    odd_s = parity[0] == 1
    odd_b = parity[1] == 1
    blk1[...] = pick(odd_s, message[2], message[0])
    blk0[...] = pick(odd_s, message[0], message[2])
    band1[...] = pick(odd_b, message[3], message[1])
    band0[...] = pick(odd_b, message[1], message[3])


def receive(parity, blk1, blk0, band1, band0):
    odd_s = parity[0] == 1
    odd_b = parity[1] == 1
    blk1, blk0, band1, band0 = blk1[...], blk0[...], band1[...], band0[...]
    return [
        pick(odd_s, blk0, blk1),
        pick(odd_b, band0, band1),
        pick(odd_s, blk1, blk0),
        pick(odd_b, band1, band0),
    ]


def first_kernel(
    parity, b, k, q, nb, valid, left, right, penalty,
    blk1, blk0, band1, band0, khi, klo, bp, qp, gal, dsum, dloc, tab,
):
    expand = (iota((SLOTS, PAIRS), 0) == (iota((SLOTS, PAIRS), 1) >> 4)).astype(f32)
    slot = dot(nb[...].astype(f32), expand)
    weight = penalty[...] * dot(valid[...].astype(f32), expand)
    crossing = slot > 3.5
    lf = left[...].astype(f32)
    rf = right[...].astype(f32)
    far = slot * 64.0 + rf
    wloc = jnp.where(crossing, 0.0, weight)
    tab[0:4] = lf
    tab[4:8] = rf
    tab[8:12] = far
    tab[12:16] = wloc
    tab[16:20] = jnp.where(crossing, weight, 0.0)

    near = []
    arrive = jnp.zeros((1, AGG * LANES), f32)
    rr = iota((AGG * LANES, PAIRS), 0)
    row = (rr >> 7) * 64 + (rr & 63)
    for a in range(AGG):
        w3 = jnp.concatenate(split3(wloc[a : a + 1]), axis=0)
        near.append(jnp.sum(dot(w3, hot_twice(lf[a : a + 1]), NT), axis=0, keepdims=True))
        hot = (row == far[a : a + 1].astype(jnp.int32)).astype(f32).astype(bf16)
        arrive = arrive + jnp.sum(dot(w3, hot, NT), axis=0, keepdims=True)
    totals = []
    for a in range(AGG):
        total = near[a] + arrive[:, a * LANES : (a + 1) * LANES]
        tab[20 + a : 21 + a] = total
        totals.append(wide(total))

    perm = permutation()
    eye = iota((LANES, LANES), 0) == iota((LANES, LANES), 1)
    diagonals = []
    for a in range(AGG):
        cuts = []
        for m in range(PAIRED):
            tile = k[a, m * LANES : (m + 1) * LANES, m * LANES : (m + 1) * LANES]
            cuts.append(jnp.sum(jnp.where(eye, tile, 0.0), axis=0, keepdims=True))
        diagonals.append(jnp.concatenate(cuts, axis=1))
    stacked = jnp.concatenate([b[a] for a in range(AGG)] + diagonals + [jnp.zeros((4, DOF), f32)], axis=0)
    turned = mm_exact(stacked, perm)
    messages = []
    pad = jnp.zeros((MROWS - MODES, DOF), f32)
    for a in range(AGG):
        load = turned[a * COLS : (a + 1) * COLS]
        bp[a] = load
        diagonal = turned[AGG * COLS + a : AGG * COLS + a + 1] + totals[a]
        dloc[a : a + 1] = diagonal
        modes = jnp.concatenate([q[a].astype(f32), pad], axis=0).astype(bf16)
        turned_modes = dot(modes, perm)
        qp[a, 0:MROWS] = turned_modes.astype(bf16)
        qp[a, MROWS:LANES] = jnp.zeros((LANES - MROWS, DOF), bf16)
        hi, lo = split2(k[a])
        khi[a] = hi
        klo[a] = lo
        projected = dot(modes, hi) + dot(modes, lo)
        wide_modes = jnp.concatenate([modes, jnp.zeros((LANES - MROWS, DOF), bf16)], axis=0)
        galerkin = mm2(projected, wide_modes, NT)
        gal[a] = galerkin
        springs = mm2(turned_modes * totals[a], qp[a], NT)
        table = jnp.concatenate(
            [lf[a : a + 1], rf[a : a + 1], jnp.where(crossing, weight, 0.0)[a : a + 1]], axis=1
        )
        fine = jnp.concatenate([load, turned_modes], axis=0)
        extra = jnp.concatenate([diagonal, table, jnp.zeros((6, DOF), f32)], axis=0)
        body = jnp.concatenate([fine, extra], axis=0)
        dsum[a] = galerkin + springs
        side = jnp.concatenate([galerkin + springs, jnp.zeros((80 - MROWS, LANES), f32)], axis=0)
        messages.append(jnp.concatenate([body, side], axis=1))
    send(parity, messages, blk1, blk0, band1, band0)


def local_kernel(khi, klo, qp, gal, tab, pkhi, pklo, ghi, glo, big):
    perm = permutation()
    back = permutation_back()
    for a in range(AGG):
        pkhi[a] = dot(back, dot(khi[a], perm).astype(bf16)).astype(bf16)
        pklo[a] = dot(back, dot(klo[a], perm).astype(bf16)).astype(bf16)
    r = iota((AGG * LANES, 2 * PAIRS), 0)
    shift = 64 * (iota((1, 2 * PAIRS), 1) >> 7)
    big[...] = jnp.zeros((AGG * LANES, AGG * LANES), f32)
    for a in range(AGG):
        l2 = jnp.concatenate([tab[a : a + 1]] * 2, axis=1).astype(jnp.int32) + shift + a * LANES
        fi = tab[8 + a : 9 + a].astype(jnp.int32)
        fi = (fi >> 6) * LANES + (fi & 63)
        f2 = jnp.concatenate([fi] * 2, axis=1) + shift
        w2 = jnp.concatenate([tab[12 + a : 13 + a]] * 2, axis=1)
        far = (r == f2).astype(f32)
        hi, mid, lo = split3(w2)
        near = (r[0:LANES] + a * LANES == l2).astype(f32)
        nb = near.astype(bf16)
        farb = far.astype(bf16)
        parts = jnp.concatenate([nb * hi, nb * mid, nb * lo], axis=0)
        m = dot(parts, farb, NT)
        m = m[0:LANES] + m[LANES : 2 * LANES] + m[2 * LANES :]
        big[a * LANES : (a + 1) * LANES, :] += m
    mm = big[...]
    adj = mm + mm.T
    eye = iota((AGG * LANES, AGG * LANES), 0) == iota((AGG * LANES, AGG * LANES), 1)
    total = jnp.concatenate([tab[20 + a : 21 + a] for a in range(AGG)], axis=1)
    lap = jnp.where(eye, total, 0.0) - adj
    gh, gl = split2(lap)
    ghi[...] = gh
    glo[...] = gl
    big[...] = jnp.zeros((AGG * LANES, AGG * LANES), f32)
    ys = []
    for a in range(AGG):
        rows = rows_of(qp[a, 0:MROWS])
        y = dot(rows, gh[a * LANES : (a + 1) * LANES]) + dot(rows, gl[a * LANES : (a + 1) * LANES])
        ys.append(y)
    for a in range(AGG):
        stacked = jnp.concatenate(
            [lanes_of(y[:, a * LANES : (a + 1) * LANES]) for y in ys], axis=0
        )
        block = mm2(stacked, qp[a], NT)
        for c in range(AGG):
            part = block[c * MROWS : (c + 1) * MROWS]
            if c == a:
                part = part + gal[a]
            big[c * LANES : c * LANES + MROWS, a * LANES : (a + 1) * LANES] = part


def crossing_kernel_values(received, tab, j):
    if j < 2:
        table = received[73:74]
        halo = table[:, 0:PAIRS]
        own = table[:, PAIRS : 2 * PAIRS]
        w = table[:, 2 * PAIRS : 3 * PAIRS]
    else:
        own = tab[j : j + 1]
        halo = tab[4 + j : 5 + j]
        w = tab[16 + j : 17 + j]
    return own, halo, w


def second_kernel(
    parity, blk1, blk0, band1, band0, bp, qp, dloc, tab, khi, klo, ghi, glo,
    oblk1, oblk0, oband1, oband0, xhi, xlo, rec, rech, qh, cdh, tco, tch, x2o, r1o, dlt, pr, pgo,
):
    halo = receive(parity, blk1, blk0, band1, band0)
    cross, crossh, xs, xh = [], [], [], []
    for j in range(AGG):
        own, far, w = crossing_kernel_values(halo[j], tab, j)
        w3 = jnp.concatenate(split3(w), axis=0)
        cross.append(wide(jnp.sum(dot(w3, hot_twice(own), NT), axis=0, keepdims=True)))
        crossh.append(wide(jnp.sum(dot(w3, hot_twice(far), NT), axis=0, keepdims=True)))
        near = hot_paired(own)
        hi, mid, lo = split3(jnp.concatenate([w, w], axis=1))
        m = dot(jnp.concatenate([near * hi, near * mid, near * lo], axis=0), hot_paired(far), NT)
        m = m[0:LANES] + m[LANES : 2 * LANES] + m[2 * LANES :]
        hi, lo = split2(m)
        xhi[j] = hi
        xlo[j] = lo
        tco[j : j + 1] = cross[j]
        tch[j : j + 1] = crossh[j]
        inverse = 1.0 / (dloc[j : j + 1] + cross[j])
        inverseh = 1.0 / (halo[j][72:73, 0:DOF] + crossh[j])
        rec[j : j + 1] = inverse
        rech[j : j + 1] = inverseh
        qh[j, 0:MROWS] = halo[j][32:72, 0:DOF].astype(bf16)
        qh[j, MROWS:LANES] = jnp.zeros((LANES - MROWS, DOF), bf16)
        cdh[j] = halo[j][0:MROWS, DOF : DOF + LANES]
        xs.append(fine_damping * inverse * bp[j])
        xh.append(fine_damping * inverseh * halo[j][0:COLS, 0:DOF])
    kh = [khi[a] for a in range(AGG)]
    kl = [klo[a] for a in range(AGG)]
    gh, gl = ghi[...], glo[...]
    y = local_product(xs, kh, kl, gh, gl, cross)
    d = []
    for j in range(AGG):
        r1 = bp[j] - y[j] + to_own(xh[j], xhi[j], xlo[j])
        step = fine_damping * rec[j : j + 1] * r1
        d.append(step)
        dlt[j] = step
        x2o[j] = xs[j] + step
        r1o[j] = r1
    y = local_product(d, kh, kl, gh, gl, cross)
    messages = []
    for j in range(AGG):
        part = r1o[j] - y[j]
        pr[j] = part
        pg = mm2(part, qp[j], NT)
        pgo[j] = pg
        messages.append(jnp.concatenate([d[j], pg], axis=1))
    send(parity, messages, oblk1, oblk0, oband1, oband0)


def inverse_kernel(
    qp, qh, dsum, cdh, tco, tch, xhi, xlo, big, inv, invh, cxhi, cxlo, chi, clo, work
):
    whole = big[...]
    ch, cl = split2(whole)
    chi[...] = ch
    clo[...] = cl
    for j in range(AGG):
        own = mm2(qp[j, 0:MROWS].astype(f32) * tco[j : j + 1], qp[j], NT)
        corner = big[j * LANES : j * LANES + MROWS, j * LANES : (j + 1) * LANES] + own
        hi, lo = split2(corner)
        chi[j * LANES : j * LANES + MROWS, j * LANES : (j + 1) * LANES] = hi
        clo[j * LANES : j * LANES + MROWS, j * LANES : (j + 1) * LANES] = lo
        other = mm2(qh[j, 0:MROWS].astype(f32) * tch[j : j + 1], qh[j], NT)
        work[:, j, :] = dsum[j] + own
        work[:, AGG + j, :] = cdh[j] + other
        rows = rows_of(qp[j, 0:MROWS])
        y = lanes_of(dot(rows, xhi[j]) + dot(rows, xlo[j]))
        hi, lo = split2(-mm2(y, qh[j], NT))
        cxhi[j, 0:MROWS] = hi
        cxlo[j, 0:MROWS] = lo
        cxhi[j, MROWS:LANES] = jnp.zeros((LANES - MROWS, LANES), bf16)
        cxlo[j, MROWS:LANES] = jnp.zeros((LANES - MROWS, LANES), bf16)
    lane = iota((8, LANES), 1)
    rows = [work[i] + jnp.where(lane == 64 + i, 1.0, 0.0) for i in range(MODES)]
    for s in range(MODES):
        pivot = jnp.broadcast_to(rows[s][:, s : s + 1], (8, LANES))
        scaled = rows[s] / pivot
        for i in range(MODES):
            if i != s:
                rows[i] = rows[i] - jnp.broadcast_to(rows[i][:, s : s + 1], (8, LANES)) * scaled
        rows[s] = scaled
    for i in range(MODES):
        work[i] = jnp.where(lane < 64, pltpu.roll(rows[i], 64, 1), 0.0)
    for i in range(MODES, MROWS):
        work[i] = jnp.zeros((8, LANES), f32)
    for j in range(AGG):
        inv[j, 0:MROWS] = work[:, j, :]
        invh[j, 0:MROWS] = work[:, AGG + j, :]
        inv[j, MROWS:LANES] = jnp.zeros((LANES - MROWS, LANES), f32)
        invh[j, MROWS:LANES] = jnp.zeros((LANES - MROWS, LANES), f32)


def coarse_local(e, chi, clo):
    y = mm3(jnp.concatenate(e, axis=1), chi, clo)
    return [y[:, a * LANES : (a + 1) * LANES] for a in range(AGG)]


def third_kernel(
    parity, blk1, blk0, band1, band0, pr, pg, dlt, qp, qh, xhi, xlo, inv, invh, chi, clo, cxhi, cxlo,
    oblk1, oblk0, oband1, oband0, r2o, e1o, d1o, pm2o,
):
    halo = receive(parity, blk1, blk0, band1, band0)
    e0, e0h, g = [], [], []
    for j in range(AGG):
        change = to_own(halo[j][:, 0:DOF], xhi[j], xlo[j])
        r2o[j] = pr[j] + change
        g.append(pg[j] + mm2(change, qp[j], NT))
        changeh = to_halo(dlt[j], xhi[j], xlo[j])
        gh = halo[j][:, DOF : DOF + LANES] + mm2(changeh, qh[j], NT)
        e0.append(coarse_damping * exact(g[j], inv[j]))
        e0h.append(coarse_damping * exact(gh, invh[j]))
    ch, cl = chi[...], clo[...]
    applied = coarse_local(e0, ch, cl)
    d1, m1 = [], []
    for j in range(AGG):
        m = g[j] - applied[j] - mm3(e0h[j], cxhi[j], cxlo[j], NT)
        m1.append(m)
        d1.append(coarse_damping * exact(m, inv[j]))
    applied = coarse_local(d1, ch, cl)
    messages = []
    for j in range(AGG):
        part = m1[j] - applied[j]
        pm2o[j] = part
        d1o[j] = d1[j]
        e1o[j] = e0[j] + d1[j]
        messages.append(jnp.concatenate([d1[j], part], axis=1))
    send(parity, messages, oblk1, oblk0, oband1, oband0)


def fourth_kernel(
    parity, blk1, blk0, band1, band0, pm2, d1, e1, inv, invh, chi, clo, cxhi, cxlo,
    x2, r2, qp, khi, klo, ghi, glo, tco,
    oblk1, oblk0, oband1, oband0, x3o, f3o, pr3o,
):
    halo = receive(parity, blk1, blk0, band1, band0)
    d2, d2h, m2 = [], [], []
    for j in range(AGG):
        m = pm2[j] - mm3(halo[j][:, 0:LANES], cxhi[j], cxlo[j], NT)
        mh = halo[j][:, LANES : 2 * LANES] - mm3(d1[j], cxhi[j], cxlo[j])
        m2.append(m)
        d2.append(coarse_damping * exact(m, inv[j]))
        d2h.append(coarse_damping * exact(mh, invh[j]))
    applied = coarse_local(d2, chi[...], clo[...])
    e, f = [], []
    for j in range(AGG):
        m = m2[j] - applied[j] - mm3(d2h[j], cxhi[j], cxlo[j], NT)
        e.append(e1[j] + d2[j] + coarse_damping * exact(m, inv[j]))
        f.append(mm2(e[j], qp[j]))
        f3o[j] = f[j]
        x3o[j] = x2[j] + f[j]
    cross = [tco[j : j + 1] for j in range(AGG)]
    y = local_product(
        f, [khi[a] for a in range(AGG)], [klo[a] for a in range(AGG)], ghi[...], glo[...], cross
    )
    messages = []
    for j in range(AGG):
        part = r2[j] - y[j]
        pr3o[j] = part
        messages.append(jnp.concatenate([part, e[j]], axis=1))
    send(parity, messages, oblk1, oblk0, oband1, oband0)


def last_kernel(
    parity, blk1, blk0, band1, band0, x3, f3, pr3, qh, rec, rech, khi, klo, ghi, glo, tco, xhi, xlo,
    field, residual,
):
    halo = receive(parity, blk1, blk0, band1, band0)
    d4, d4h, r3 = [], [], []
    for j in range(AGG):
        fh = mm2(halo[j][:, DOF : DOF + LANES], qh[j])
        r = pr3[j] + to_own(fh, xhi[j], xlo[j])
        rh = halo[j][:, 0:DOF] + to_halo(f3[j], xhi[j], xlo[j])
        r3.append(r)
        d4.append(fine_damping * rec[j : j + 1] * r)
        d4h.append(fine_damping * rech[j : j + 1] * rh)
    cross = [tco[j : j + 1] for j in range(AGG)]
    y = local_product(
        d4, [khi[a] for a in range(AGG)], [klo[a] for a in range(AGG)], ghi[...], glo[...], cross
    )
    out = []
    for j in range(AGG):
        out.append(x3[j] + d4[j])
    for j in range(AGG):
        out.append(r3[j] - y[j] + to_own(d4h[j], xhi[j], xlo[j]))
    turned = mm_exact(jnp.concatenate(out, axis=0), permutation_back())
    for j in range(AGG):
        field[j] = turned[j * COLS : (j + 1) * COLS]
        residual[j] = turned[(AGG + j) * COLS : (AGG + j + 1) * COLS]


VM = pl.BlockSpec(memory_space=pltpu.VMEM)
SM = pl.BlockSpec(memory_space=pltpu.SMEM)


def run(kernel, outs, *args, scalars=0, scratch=()):
    return pl.pallas_call(
        kernel,
        out_shape=[jax.ShapeDtypeStruct(shape, kind) for shape, kind in outs],
        in_specs=[SM] * scalars + [VM] * (len(args) - scalars),
        out_specs=[VM] * len(outs),
        scratch_shapes=list(scratch),
        compiler_params=pltpu.CompilerParams(vmem_limit_bytes=24 * 2**20),
    )(*args)


def swapped(x, axis, odd):
    length = lax.axis_size(axis)
    route = []
    for i in range(odd, length + odd, 2):
        near, far = i % length, (i + 1) % length
        route += [(near, far), (far, near)]
    return lax.ppermute(x, axis, route)


def exchange(messages):
    blk1, blk0, band1, band0 = messages
    in0 = swapped(band0, "band", 0)
    in1 = swapped(band1, "band", 1)
    in2 = swapped(blk0, "blk", 0)
    in3 = swapped(blk1, "blk", 1)
    return in3, in2, in1, in0


def shards(
    load_columns, stiffness, rigid_modes, neighbours, slot_valid, pair_left, pair_right, penalty
):
    parity = jnp.stack([lax.axis_index("blk") % 2, lax.axis_index("band") % 2]).astype(jnp.int32)
    fields = ((AGG, COLS, DOF), f32)
    modes = ((AGG, LANES, DOF), bf16)
    square = ((AGG, DOF, DOF), bf16)
    local = ((AGG * LANES, AGG * LANES), bf16)
    small = ((AGG, MROWS, LANES), f32)
    tile = ((AGG, LANES, LANES), bf16)
    tile32 = ((AGG, LANES, LANES), f32)
    rows = ((AGG, DOF), f32)
    coarse = ((AGG, COLS, LANES), f32)

    def message(height, width):
        return [((height, width), f32)] * 4

    *out, khi, klo, bp, qp, gal, dsum, dloc, tab = run(
        first_kernel,
        message(80, DOF + LANES)
        + [square, square, fields, modes, small, small, rows, ((24, PAIRS), f32)],
        parity,
        load_columns[0, 0],
        stiffness[0, 0],
        rigid_modes[0, 0],
        neighbours[0, 0],
        slot_valid[0, 0],
        pair_left[0, 0],
        pair_right[0, 0],
        penalty[0, 0],
        scalars=1,
    )
    got = exchange(out)
    pkhi, pklo, ghi, glo, big = run(
        local_kernel,
        [square, square, local, local, ((AGG * LANES, AGG * LANES), f32)],
        khi, klo, qp, gal, tab,
    )
    *out, xhi, xlo, rec, rech, qh, cdh, tco, tch, x2, r1, dlt, pr, pg = run(
        second_kernel,
        message(COLS, DOF + LANES)
        + [tile, tile, rows, rows, modes, small, rows, rows, fields, fields, fields, fields, coarse],
        parity, *got, bp, qp, dloc, tab, pkhi, pklo, ghi, glo,
        scalars=1,
    )
    got = exchange(out)
    inv, invh, cxhi, cxlo, chi, clo = run(
        inverse_kernel,
        [tile32, tile32, tile, tile, local, local],
        qp, qh, dsum, cdh, tco, tch, xhi, xlo, big,
        scratch=[pltpu.VMEM((MROWS, 2 * AGG, LANES), f32)],
    )
    *out, r2, e1, d1, pm2 = run(
        third_kernel,
        message(COLS, 2 * LANES) + [fields, coarse, coarse, coarse],
        parity, *got, pr, pg, dlt, qp, qh, xhi, xlo, inv, invh, chi, clo, cxhi, cxlo,
        scalars=1,
    )
    got = exchange(out)
    *out, x3, f3, pr3 = run(
        fourth_kernel,
        message(COLS, DOF + LANES) + [fields, fields, fields],
        parity, *got, pm2, d1, e1, inv, invh, chi, clo, cxhi, cxlo,
        x2, r2, qp, pkhi, pklo, ghi, glo, tco,
        scalars=1,
    )
    got = exchange(out)
    field, residual = run(
        last_kernel,
        [fields, fields],
        parity, *got, x3, f3, pr3, qh, rec, rech, pkhi, pklo, ghi, glo, tco, xhi, xlo,
        scalars=1,
    )
    return (field[None, None], residual[None, None])


def solution(mesh):
    in_specs = (
        P("band", "blk", None, None, None),
        P("band", "blk", None, None, None),
        P("band", "blk", None, None, None),
        P("band", "blk", None, None),
        P("band", "blk", None, None),
        P("band", "blk", None, None),
        P("band", "blk", None, None),
        P("band", "blk", None, None),
    )
    out_specs = (P("band", "blk", None, None, None), P("band", "blk", None, None, None))
    return jax.shard_map(shards, mesh=mesh, in_specs=in_specs, out_specs=out_specs, check_vma=False)
```

```python
import jax
import jax.numpy as jnp
from jax import lax
from jax.experimental import pallas as pl
from jax.experimental.pallas import tpu as pltpu
from jax.sharding import PartitionSpec as P

COLS = 32
BLOCKS = 64
DOF = 384
MODES = 36
SLOTS = 8
PAIRS = 128
AGG = 4
LANES = 128
PAIRED = 3
STRIDE = 64
WIDTH = AGG * STRIDE

fine_damping = 0.6
coarse_damping = 0.7
f32 = jnp.float32
bf16 = jnp.bfloat16

NN = (((1,), (0,)), ((), ()))
NT = (((1,), (1,)), ((), ()))


def dot(a, b, dims=NN):
    return lax.dot_general(a, b, dims, preferred_element_type=f32)


def split2(x):
    hi = x.astype(bf16)
    lo = (x - hi.astype(f32)).astype(bf16)
    return hi, lo


def split3(x):
    hi = x.astype(bf16)
    rest = x - hi.astype(f32)
    mid = rest.astype(bf16)
    lo = (rest - mid.astype(f32)).astype(bf16)
    return hi, mid, lo


def mm3(x, whi, wlo, dims=NN):
    rows = x.shape[0]
    hi, lo = split2(x)
    first = dot(jnp.concatenate([hi, lo], axis=0), whi, dims)
    return first[:rows] + first[rows:] + dot(hi, wlo, dims)


def mm2(x, w, dims=NN):
    rows = x.shape[0]
    hi, lo = split2(x)
    both = dot(jnp.concatenate([hi, lo], axis=0), w, dims)
    return both[:rows] + both[rows:]


def mm_exact(x, w, dims=NN):
    rows = x.shape[0]
    parts = dot(jnp.concatenate(split3(x), axis=0), w, dims)
    return parts[:rows] + parts[rows : 2 * rows] + parts[2 * rows :]


def iota(shape, axis):
    return lax.broadcasted_iota(jnp.int32, shape, axis)


def permutation():
    i = iota((DOF, DOF), 0)
    j = iota((DOF, DOF), 1)
    return (i == 6 * (j & 63) + (j >> 6)).astype(f32).astype(bf16)


def permutation_back():
    i = iota((DOF, DOF), 0)
    j = iota((DOF, DOF), 1)
    return (j == 6 * (i & 63) + (i >> 6)).astype(f32).astype(bf16)


def hot_twice(index):
    k = iota((LANES, PAIRS), 0) & 63
    return (k == index.astype(jnp.int32)).astype(f32).astype(bf16)


def hot_paired(index):
    r = iota((LANES, 2 * PAIRS), 0)
    doubled = jnp.concatenate([index.astype(jnp.int32)] * 2, axis=1)
    want = doubled + 64 * (iota((1, 2 * PAIRS), 1) >> 7)
    return (r == want).astype(f32).astype(bf16)


def wide(t):
    return jnp.concatenate([t] * PAIRED, axis=1)


def stack_fields(v):
    rows = []
    for m in range(PAIRED):
        rows.append(jnp.concatenate([x[:, m * LANES : (m + 1) * LANES] for x in v], axis=1))
    return jnp.concatenate(rows, axis=0)


def unstack_fields(y, count):
    out = []
    for a in range(count):
        parts = [
            y[m * COLS : (m + 1) * COLS, a * LANES : (a + 1) * LANES] for m in range(PAIRED)
        ]
        out.append(jnp.concatenate(parts, axis=1))
    return out


def rows_of(x):
    return jnp.concatenate([x[:, m * LANES : (m + 1) * LANES] for m in range(PAIRED)], axis=0)


def lanes_of(x):
    r = x.shape[0] // PAIRED
    return jnp.concatenate([x[m * r : (m + 1) * r] for m in range(PAIRED)], axis=1)


def local_product(v, khi, klo, ghi, glo, cross):
    springs = unstack_fields(mm3(stack_fields(v), ghi, glo), AGG)
    return [
        mm3(v[a], khi[a], klo[a]) + (springs[a] + v[a] * cross[a]) for a in range(AGG)
    ]


def to_own(vh, xhi, xlo):
    return lanes_of(mm3(rows_of(vh), xhi, xlo, NT))


def to_halo(v, xhi, xlo):
    return lanes_of(mm3(rows_of(v), xhi, xlo))


def pick(flag, a, b):
    return jnp.where(flag, a, b)


def send(parity, message, blk1, blk0, band1, band0):
    odd_s = parity[0] == 1
    odd_b = parity[1] == 1
    blk1[...] = pick(odd_s, message[2], message[0])
    blk0[...] = pick(odd_s, message[0], message[2])
    band1[...] = pick(odd_b, message[3], message[1])
    band0[...] = pick(odd_b, message[1], message[3])


def receive(parity, blk1, blk0, band1, band0):
    odd_s = parity[0] == 1
    odd_b = parity[1] == 1
    blk1, blk0, band1, band0 = blk1[...], blk0[...], band1[...], band0[...]
    return [
        pick(odd_s, blk0, blk1),
        pick(odd_b, band0, band1),
        pick(odd_s, blk1, blk0),
        pick(odd_b, band1, band0),
    ]


def block_diagonal(blocks):
    rows = []
    for j in range(AGG):
        parts = []
        if j > 0:
            parts.append(jnp.zeros((STRIDE, j * STRIDE), f32))
        parts.append(blocks[j])
        if j < AGG - 1:
            parts.append(jnp.zeros((STRIDE, (AGG - 1 - j) * STRIDE), f32))
        rows.append(jnp.concatenate(parts, axis=1))
    return jnp.concatenate(rows, axis=0)


def store2(hi_ref, lo_ref, x):
    hi, lo = split2(x)
    hi_ref[...] = hi
    lo_ref[...] = lo


def sent_modes(sent):
    pad = jnp.zeros((STRIDE - MODES, DOF), f32)
    return jnp.concatenate([sent[32:68], pad], axis=0).astype(bf16)


def sent_diagonal(sent):
    tail = sent[72:80]
    return jnp.concatenate([tail[:, t * STRIDE : (t + 1) * STRIDE] for t in range(5)], axis=0)


def pair_weights(own, far, w, xhi, xlo, j):
    w3 = jnp.concatenate(split3(w), axis=0)
    total = wide(jnp.sum(dot(w3, hot_twice(own), NT), axis=0, keepdims=True))
    total_far = wide(jnp.sum(dot(w3, hot_twice(far), NT), axis=0, keepdims=True))
    near = hot_paired(own)
    hi, mid, lo = split3(jnp.concatenate([w, w], axis=1))
    m = dot(jnp.concatenate([near * hi, near * mid, near * lo], axis=0), hot_paired(far), NT)
    m = m[0:LANES] + m[LANES : 2 * LANES] + m[2 * LANES :]
    hi, lo = split2(m)
    xhi[j] = hi
    xlo[j] = lo
    return total, total_far


def first_kernel(
    parity, b_in, k_in, q_in, nb_in, valid_in, left_in, right_in, penalty_in,
    blk1, blk0, band1, band0, tab,
    b, k, q, nb, valid, left, right, penalty, sem,
):
    small = [
        pltpu.make_async_copy(src, dst, sem.at[n])
        for n, (src, dst) in enumerate(
            [
                (nb_in, nb),
                (valid_in, valid),
                (left_in, left),
                (right_in, right),
                (penalty_in, penalty),
                (q_in, q),
                (b_in, b),
            ]
        )
    ]
    large = [pltpu.make_async_copy(k_in.at[a], k.at[a], sem.at[8 + a]) for a in range(AGG)]
    for copy in small + large:
        copy.start()
    perm = permutation()
    for copy in small:
        copy.wait()

    expand = (iota((SLOTS, PAIRS), 0) == (iota((SLOTS, PAIRS), 1) >> 4)).astype(f32)
    slot = dot(nb[...].astype(f32), expand)
    weight = penalty[...] * dot(valid[...].astype(f32), expand)
    crossing = slot > 3.5
    lf = left[...].astype(f32)
    rf = right[...].astype(f32)
    far = slot * 64.0 + rf
    wloc = jnp.where(crossing, 0.0, weight)
    wcross = jnp.where(crossing, weight, 0.0)
    tab[0:4] = lf
    tab[4:8] = rf
    tab[8:12] = far
    tab[12:16] = wloc
    tab[16:20] = wcross

    near = []
    arrive = jnp.zeros((1, AGG * LANES), f32)
    rr = iota((AGG * LANES, PAIRS), 0)
    row = (rr >> 7) * 64 + (rr & 63)
    for a in range(AGG):
        w3 = jnp.concatenate(split3(wloc[a : a + 1]), axis=0)
        near.append(jnp.sum(dot(w3, hot_twice(lf[a : a + 1]), NT), axis=0, keepdims=True))
        hot = (row == far[a : a + 1].astype(jnp.int32)).astype(f32).astype(bf16)
        arrive = arrive + jnp.sum(dot(w3, hot, NT), axis=0, keepdims=True)
    totals = []
    for a in range(AGG):
        total = near[a] + arrive[:, a * LANES : (a + 1) * LANES]
        tab[20 + a : 21 + a] = total
        totals.append(wide(total))

    pad = jnp.zeros((STRIDE - MODES, DOF), f32)
    q_all = q[...].astype(f32)
    modes = [jnp.concatenate([q_all[:, a, :], pad], axis=0).astype(bf16) for a in range(AGG)]
    turned_modes = dot(jnp.concatenate(modes, axis=0), perm)
    turned_modes = [turned_modes[a * STRIDE : (a + 1) * STRIDE] for a in range(AGG)]
    eye = iota((LANES, LANES), 0) == iota((LANES, LANES), 1)
    diagonals = []
    for a in range(AGG):
        large[a].wait()
        cuts = []
        for m in range(PAIRED):
            tile = k[a, m * LANES : (m + 1) * LANES, m * LANES : (m + 1) * LANES]
            cuts.append(jnp.sum(jnp.where(eye, tile, 0.0), axis=0, keepdims=True))
        diagonals.append(jnp.concatenate(cuts, axis=1))
    stacked = jnp.concatenate(
        [b[a] for a in range(AGG)] + diagonals + [jnp.zeros((4, DOF), f32)], axis=0
    )
    turned = mm_exact(stacked, perm)
    messages = []
    for a in range(AGG):
        load = turned[a * COLS : (a + 1) * COLS]
        diagonal = turned[AGG * COLS + a : AGG * COLS + a + 1] + totals[a]
        hi, lo = split2(k[a])
        projected = dot(modes[a], hi) + dot(modes[a], lo)
        galerkin = mm2(projected, modes[a], NT)
        whole = galerkin + mm2(turned_modes[a] * totals[a], turned_modes[a].astype(bf16), NT)
        table = jnp.concatenate([lf[a : a + 1], rf[a : a + 1], wcross[a : a + 1]], axis=1)
        side = [whole[8 * t : 8 * t + 8] for t in range(5)] + [jnp.zeros((8, STRIDE), f32)]
        messages.append(
            jnp.concatenate(
                [
                    load,
                    turned_modes[a][0:32],
                    jnp.concatenate([turned_modes[a][32:36], diagonal, table], axis=0),
                    jnp.zeros((2, DOF), f32),
                    jnp.concatenate(side, axis=1),
                ],
                axis=0,
            )
        )
    send(parity, messages, blk1, blk0, band1, band0)


def local_kernel(
    parity, blk1, blk0, band1, band0, k, tab,
    pkhi, pklo, ghi, glo, aqhi, aqlo, big, xhi, xlo, tco, tch, bp, qp, dsum, dloc, work,
):
    for a, sent in enumerate(receive(parity, blk1, blk0, band1, band0)):
        bp[a] = sent[0:COLS]
        qp[a] = sent_modes(sent)
        dsum[a] = sent_diagonal(sent)
        dloc[a : a + 1] = sent[68:69]
    perm = permutation()
    back = permutation_back()
    for a in range(AGG):
        hi, lo = split2(k[a])
        pkhi[a] = dot(back, dot(hi, perm).astype(bf16)).astype(bf16)
        pklo[a] = dot(back, dot(lo, perm).astype(bf16)).astype(bf16)
    r = iota((AGG * LANES, 2 * PAIRS), 0)
    shift = 64 * (iota((1, 2 * PAIRS), 1) >> 7)
    rows = []
    for a in range(AGG):
        fi = tab[8 + a : 9 + a].astype(jnp.int32)
        fi = (fi >> 6) * LANES + (fi & 63)
        f2 = jnp.concatenate([fi] * 2, axis=1) + shift
        w2 = jnp.concatenate([tab[12 + a : 13 + a]] * 2, axis=1)
        far = (r == f2).astype(f32).astype(bf16)
        hi, mid, lo = split3(w2)
        near = hot_paired(tab[a : a + 1])
        parts = jnp.concatenate([near * hi, near * mid, near * lo], axis=0)
        m = dot(parts, far, NT)
        rows.append(m[0:LANES] + m[LANES : 2 * LANES] + m[2 * LANES :])
    mm = jnp.concatenate(rows, axis=0)
    work[...] = mm + mm.T
    eye = iota((AGG * LANES, AGG * LANES), 0) == iota((AGG * LANES, AGG * LANES), 1)
    total = jnp.concatenate([tab[20 + a : 21 + a] for a in range(AGG)], axis=1)
    gh, gl = split2(jnp.where(eye, total, 0.0) - work[...])
    ghi[...] = gh
    glo[...] = gl
    lines = []
    for a in range(AGG):
        rows = rows_of(qp[a].astype(f32)).astype(bf16)
        y = dot(rows, gh[a * LANES : (a + 1) * LANES]) + dot(rows, gl[a * LANES : (a + 1) * LANES])
        turned = dot(qp[a], pkhi[a]) + dot(qp[a], pklo[a])
        parts = []
        for c in range(AGG):
            part = lanes_of(y[:, c * LANES : (c + 1) * LANES])
            parts.append(part + turned if c == a else part)
        lines.append(jnp.concatenate(parts, axis=1))
    aq = jnp.concatenate(lines, axis=0)
    ah, al = split2(aq)
    aqhi[...] = ah
    aqlo[...] = al
    columns = []
    for a in range(AGG):
        both = jnp.concatenate([ah, al], axis=0)[:, a * DOF : (a + 1) * DOF]
        block = dot(both, qp[a], NT)
        columns.append(block[:WIDTH] + block[WIDTH:])
    big[...] = jnp.concatenate(columns, axis=1)
    for j in range(2, AGG):
        tco[j : j + 1], tch[j : j + 1] = pair_weights(
            tab[j : j + 1], tab[4 + j : 5 + j], tab[16 + j : 17 + j], xhi, xlo, j - 2
        )
    tco[0:2] = jnp.zeros((2, DOF), f32)
    tch[0:2] = jnp.zeros((2, DOF), f32)


def second_kernel(
    parity, blk1, blk0, band1, band0, bp, qp, dloc, khi, klo, ghi, glo, aqhi, aqlo, x2hi, x2lo, t2o, t2h,
    oblk1, oblk0, oband1, oband0, xhi, xlo, rec, rech, qh, cdh, tco, tch, x2o, r1o, dlt, pgo,
):
    halo = receive(parity, blk1, blk0, band1, band0)
    cross, xs, xh = [], [], []
    for j in range(AGG):
        if j < 2:
            table = halo[j][69:70]
            total, total_far = pair_weights(
                table[:, PAIRS : 2 * PAIRS], table[:, 0:PAIRS], table[:, 2 * PAIRS :], xhi, xlo, j
            )
        else:
            xhi[j] = x2hi[j - 2]
            xlo[j] = x2lo[j - 2]
            total, total_far = t2o[j : j + 1], t2h[j : j + 1]
        cross.append(total)
        tco[j : j + 1] = total
        tch[j : j + 1] = total_far
        inverse = fine_damping / (dloc[j : j + 1] + total)
        inverseh = fine_damping / (halo[j][68:69] + total_far)
        rec[j : j + 1] = inverse
        rech[j : j + 1] = inverseh
        qh[j] = sent_modes(halo[j])
        cdh[j] = sent_diagonal(halo[j])
        xs.append(inverse * bp[j])
        xh.append(inverseh * halo[j][0:COLS])
    kh = [khi[a] for a in range(AGG)]
    kl = [klo[a] for a in range(AGG)]
    y = local_product(xs, kh, kl, ghi[...], glo[...], cross)
    d, pg = [], []
    for j in range(AGG):
        r1 = bp[j] - y[j] + to_own(xh[j], xhi[j], xlo[j])
        step = rec[j : j + 1] * r1
        d.append(step)
        dlt[j] = step
        x2o[j] = xs[j] + step
        r1o[j] = r1
        pg.append(mm2(r1 - step * cross[j], qp[j], NT))
    pg = jnp.concatenate(pg, axis=1) - mm3(jnp.concatenate(d, axis=1), aqhi[...], aqlo[...], NT)
    pgo[...] = pg
    messages = []
    for j in range(AGG):
        part = pg[:, j * STRIDE : (j + 1) * STRIDE]
        messages.append(jnp.concatenate([d[j], part, jnp.zeros((COLS, STRIDE), f32)], axis=1))
    send(parity, messages, oblk1, oblk0, oband1, oband0)


def inverse_kernel(
    dlt, r1, khi, klo, ghi, glo, qp, qh, dsum, cdh, tco, tch, xhi, xlo, big,
    pr, yhi, ylo, zhi, zlo, ghp, hhi, hlo, hhhi, hhlo, gchi, gclo, gxhi, gxlo, gohi, golo, work,
):
    d = [dlt[j] for j in range(AGG)]
    cross = [tco[j : j + 1] for j in range(AGG)]
    y = local_product(
        d, [khi[a] for a in range(AGG)], [klo[a] for a in range(AGG)], ghi[...], glo[...], cross
    )
    for j in range(AGG):
        pr[j] = r1[j] - y[j]
    corner, couple, part = [], [], []
    for j in range(AGG):
        mine = qp[j].astype(f32)
        other = qh[j].astype(f32)
        rows = rows_of(mine).astype(bf16)
        y = lanes_of(dot(rows, xhi[j]) + dot(rows, xlo[j]))
        hi, lo = split2(y)
        yhi[j] = hi
        ylo[j] = lo
        couple.append(-(dot(hi, qh[j], NT) + dot(lo, qh[j], NT)))
        rows = rows_of(other).astype(bf16)
        z = lanes_of(dot(rows, xhi[j], NT) + dot(rows, xlo[j], NT))
        hi, lo = split2(z)
        zhi[j] = hi
        zlo[j] = lo
        part.append(mm3(d[j], hi, lo, NT))
        own = mm2(mine * tco[j : j + 1], qp[j], NT)
        corner.append(own)
        blank = jnp.zeros((MODES, LANES - STRIDE), f32)
        work[:, j, :] = jnp.concatenate([dsum[j][0:MODES] + own[0:MODES], blank], axis=1)
        far = mm2(other * tch[j : j + 1], qh[j], NT)
        work[:, AGG + j, :] = jnp.concatenate([cdh[j][0:MODES] + far[0:MODES], blank], axis=1)
    ghp[...] = jnp.concatenate(part, axis=1)
    lane = iota((8, LANES), 1)
    rows = [work[i] + jnp.where(lane == STRIDE + i, 1.0, 0.0) for i in range(MODES)]
    for s in range(MODES):
        pivot = jnp.broadcast_to(rows[s][:, s : s + 1], (8, LANES))
        scaled = rows[s] / pivot
        for i in range(MODES):
            if i != s:
                rows[i] = rows[i] - jnp.broadcast_to(rows[i][:, s : s + 1], (8, LANES)) * scaled
        rows[s] = scaled
    for i in range(MODES):
        work[i] = rows[i] * coarse_damping
    below = jnp.zeros((STRIDE - MODES, STRIDE), f32)
    blocks = [
        jnp.concatenate([work[:, m, :][:, STRIDE:], below], axis=0) for m in range(2 * AGG)
    ]
    hh, hl = split2(block_diagonal(blocks[:AGG]))
    hhi[...] = hh
    hlo[...] = hl
    fh, fl = split2(block_diagonal(blocks[AGG:]))
    hhhi[...] = fh
    hhlo[...] = fl
    eye = iota((WIDTH, WIDTH), 0) == iota((WIDTH, WIDTH), 1)
    whole = big[...] + block_diagonal(corner)
    store2(gchi, gclo, jnp.where(eye, 1.0, 0.0) - mm3(whole, hh, hl))
    store2(gxhi, gxlo, -mm3(block_diagonal([c.T for c in couple]), hh, hl))
    store2(gohi, golo, -mm3(block_diagonal(couple), fh, fl))


def halo_modes(halo, at):
    return jnp.concatenate([h[:, at : at + STRIDE] for h in halo], axis=1)


def third_kernel(
    parity, blk1, blk0, band1, band0, pg, ghp, yhi, ylo, hhi, hlo, hhhi, hhlo, gchi, gclo, gxhi, gxlo,
    oblk1, oblk0, oband1, oband0, e1o, d1o, p2o, dh,
):
    halo = receive(parity, blk1, blk0, band1, band0)
    parts = []
    for j in range(AGG):
        value = halo[j][:, 0:DOF]
        dh[j] = value
        parts.append(mm3(value, yhi[j], ylo[j], NT))
    g = pg[...] + jnp.concatenate(parts, axis=1)
    gh = halo_modes(halo, DOF) + ghp[...]
    e0 = mm3(g, hhi[...], hlo[...])
    e0h = mm3(gh, hhhi[...], hhlo[...])
    gch, gcl = gchi[...], gclo[...]
    d1 = mm3(e0, gch, gcl) + mm3(e0h, gxhi[...], gxlo[...])
    p2 = mm3(d1, gch, gcl)
    e1o[...] = e0 + d1
    d1o[...] = d1
    p2o[...] = p2
    messages = []
    for j in range(AGG):
        cut = slice(j * STRIDE, (j + 1) * STRIDE)
        messages.append(jnp.concatenate([d1[:, cut], p2[:, cut]], axis=1))
    send(parity, messages, oblk1, oblk0, oband1, oband0)


def beside_third_kernel(dh, pr, xhi, xlo, d1, gohi, golo, r2o, w2o):
    w2o[...] = mm3(d1[...], gohi[...], golo[...])
    for j in range(AGG):
        r2o[j] = pr[j] + to_own(dh[j], xhi[j], xlo[j])


def fourth_kernel(
    parity, blk1, blk0, band1, band0, p2, w2, e1, gchi, gclo, gxhi, gxlo, r2, qp, aqhi, aqlo, tco,
    oblk1, oblk0, oband1, oband0, eo, f3o, pr3o,
):
    halo = receive(parity, blk1, blk0, band1, band0)
    gxh, gxl = gxhi[...], gxlo[...]
    d2 = p2[...] + mm3(halo_modes(halo, 0), gxh, gxl)
    d2h = halo_modes(halo, STRIDE) + w2[...]
    d3 = mm3(d2, gchi[...], gclo[...]) + mm3(d2h, gxh, gxl)
    e = e1[...] + d2 + d3
    eo[...] = e
    y = mm3(e, aqhi[...], aqlo[...])
    messages = []
    for j in range(AGG):
        mine = e[:, j * STRIDE : (j + 1) * STRIDE]
        f = mm2(mine, qp[j])
        f3o[j] = f
        part = r2[j] - y[:, j * DOF : (j + 1) * DOF] - f * tco[j : j + 1]
        pr3o[j] = part
        messages.append(jnp.concatenate([part, mine, jnp.zeros((COLS, STRIDE), f32)], axis=1))
    send(parity, messages, oblk1, oblk0, oband1, oband0)


def beside_fourth_kernel(e, x2, f3, yhi, ylo, x3o, rho):
    for j in range(AGG):
        x3o[j] = x2[j] + f3[j]
        rho[j] = mm3(e[:, j * STRIDE : (j + 1) * STRIDE], yhi[j], ylo[j])


def last_kernel(
    parity, blk1, blk0, band1, band0, x3, pr3, rh3, zhi, zlo, rec, rech, khi, klo, ghi, glo, tco, xhi, xlo,
    field, residual,
):
    halo = receive(parity, blk1, blk0, band1, band0)
    d4, d4h, r3 = [], [], []
    for j in range(AGG):
        r = pr3[j] + mm3(halo[j][:, DOF : DOF + STRIDE], zhi[j], zlo[j])
        rh = halo[j][:, 0:DOF] + rh3[j]
        r3.append(r)
        d4.append(rec[j : j + 1] * r)
        d4h.append(rech[j : j + 1] * rh)
    cross = [tco[j : j + 1] for j in range(AGG)]
    y = local_product(
        d4, [khi[a] for a in range(AGG)], [klo[a] for a in range(AGG)], ghi[...], glo[...], cross
    )
    out = []
    for j in range(AGG):
        out.append(x3[j] + d4[j])
    for j in range(AGG):
        out.append(r3[j] - y[j] + to_own(d4h[j], xhi[j], xlo[j]))
    turned = mm_exact(jnp.concatenate(out, axis=0), permutation_back())
    for j in range(AGG):
        field[j] = turned[j * COLS : (j + 1) * COLS]
        residual[j] = turned[(AGG + j) * COLS : (AGG + j + 1) * COLS]


VM = pl.BlockSpec(memory_space=pltpu.VMEM)
SM = pl.BlockSpec(memory_space=pltpu.SMEM)
HB = pl.BlockSpec(memory_space=pltpu.HBM)


def run(kernel, outs, *args, scalars=0, scratch=(), place=VM, limit=24):
    if place is HB:
        args = args[:scalars] + tuple(
            pltpu.with_memory_space_constraint(x, pltpu.HBM) for x in args[scalars:]
        )
    return pl.pallas_call(
        kernel,
        out_shape=[jax.ShapeDtypeStruct(shape, kind) for shape, kind in outs],
        in_specs=[SM] * scalars + [place] * (len(args) - scalars),
        out_specs=[VM] * len(outs),
        scratch_shapes=list(scratch),
        compiler_params=pltpu.CompilerParams(vmem_limit_bytes=int(limit * 2**20)),
    )(*args)


def swapped(x, axis, odd):
    length = lax.axis_size(axis)
    route = []
    for i in range(odd, length + odd, 2):
        near, far = i % length, (i + 1) % length
        route += [(near, far), (far, near)]
    return lax.ppermute(x, axis, route)


def exchange(messages):
    blk1, blk0, band1, band0 = messages
    in0 = swapped(band0, "band", 0)
    in1 = swapped(band1, "band", 1)
    in2 = swapped(blk0, "blk", 0)
    in3 = swapped(blk1, "blk", 1)
    return in3, in2, in1, in0


def shards(
    load_columns, stiffness, rigid_modes, neighbours, slot_valid, pair_left, pair_right, penalty
):
    parity = jnp.stack([lax.axis_index("blk") % 2, lax.axis_index("band") % 2]).astype(jnp.int32)
    fields = ((AGG, COLS, DOF), f32)
    modes = ((AGG, STRIDE, DOF), bf16)
    square = ((AGG, DOF, DOF), bf16)
    local = ((AGG * LANES, AGG * LANES), bf16)
    small = ((AGG, 40, STRIDE), f32)
    tile = ((AGG, LANES, LANES), bf16)
    rows = ((AGG, DOF), f32)
    coarse = ((COLS, WIDTH), f32)
    broad = ((WIDTH, AGG * DOF), bf16)
    dense = ((WIDTH, WIDTH), bf16)

    def message(height, width):
        return [((height, width), f32)] * 4

    *out, tab = run(
        first_kernel,
        message(80, DOF) + [((24, PAIRS), f32)],
        parity,
        load_columns[0, 0],
        stiffness[0, 0],
        jnp.transpose(rigid_modes[0, 0], (1, 0, 2)),
        neighbours[0, 0],
        slot_valid[0, 0],
        pair_left[0, 0],
        pair_right[0, 0],
        penalty[0, 0],
        scalars=1,
        place=HB,
        scratch=[
            pltpu.VMEM((AGG, COLS, DOF), f32),
            pltpu.VMEM((AGG, DOF, DOF), f32),
            pltpu.VMEM((MODES, AGG, DOF), bf16),
            pltpu.VMEM((AGG, SLOTS), jnp.int32),
            pltpu.VMEM((AGG, SLOTS), jnp.int32),
            pltpu.VMEM((AGG, PAIRS), jnp.int32),
            pltpu.VMEM((AGG, PAIRS), jnp.int32),
            pltpu.VMEM((AGG, PAIRS), f32),
            pltpu.SemaphoreType.DMA((12,)),
        ],
    )
    got = exchange(out)
    pair_tile = ((2, LANES, LANES), bf16)
    pkhi, pklo, ghi, glo, aqhi, aqlo, big, x2hi, x2lo, t2o, t2h, bp, qp, dsum, dloc = run(
        local_kernel,
        [square, square, local, local, broad, broad, ((WIDTH, WIDTH), f32), pair_tile, pair_tile, rows, rows]
        + [fields, modes, small, rows],
        parity, *out, stiffness[0, 0], tab,
        scalars=1,
        scratch=[pltpu.VMEM((AGG * LANES, AGG * LANES), f32)],
    )
    *out, xhi, xlo, rec, rech, qh, cdh, tco, tch, x2, r1, dlt, pg = run(
        second_kernel,
        message(COLS, DOF + LANES)
        + [tile, tile, rows, rows, modes, small, rows, rows, fields, fields, fields, coarse],
        parity, *got, bp, qp, dloc, pkhi, pklo, ghi, glo, aqhi, aqlo, x2hi, x2lo, t2o, t2h,
        scalars=1,
    )
    got = exchange(out)
    pr, yhi, ylo, zhi, zlo, ghp, hhi, hlo, hhhi, hhlo, gchi, gclo, gxhi, gxlo, gohi, golo = run(
        inverse_kernel,
        [fields, modes, modes, modes, modes, coarse] + [dense] * 10,
        dlt, r1, pkhi, pklo, ghi, glo, qp, qh, dsum, cdh, tco, tch, xhi, xlo, big,
        scratch=[pltpu.VMEM((MODES, 2 * AGG, LANES), f32)],
    )
    *out, e1, d1, p2, dh = run(
        third_kernel,
        message(COLS, LANES) + [coarse, coarse, coarse, fields],
        parity, *got, pg, ghp, yhi, ylo, hhi, hlo, hhhi, hhlo, gchi, gclo, gxhi, gxlo,
        scalars=1,
    )
    got = exchange(out)
    r2, w2 = run(beside_third_kernel, [fields, coarse], dh, pr, xhi, xlo, d1, gohi, golo)
    *out, e, f3, pr3 = run(
        fourth_kernel,
        message(COLS, DOF + LANES) + [coarse, fields, fields],
        parity, *got, p2, w2, e1, gchi, gclo, gxhi, gxlo, r2, qp, aqhi, aqlo, tco,
        scalars=1,
    )
    got = exchange(out)
    x3, rh3 = run(beside_fourth_kernel, [fields, fields], e, x2, f3, yhi, ylo)
    field, residual = run(
        last_kernel,
        [fields, fields],
        parity, *got, x3, pr3, rh3, zhi, zlo, rec, rech, pkhi, pklo, ghi, glo, tco, xhi, xlo,
        scalars=1,
    )
    return (field[None, None], residual[None, None])


def solution(mesh):
    in_specs = (
        P("band", "blk", None, None, None),
        P("band", "blk", None, None, None),
        P("band", "blk", None, None, None),
        P("band", "blk", None, None),
        P("band", "blk", None, None),
        P("band", "blk", None, None),
        P("band", "blk", None, None),
        P("band", "blk", None, None),
    )
    out_specs = (P("band", "blk", None, None, None), P("band", "blk", None, None, None))
    return jax.shard_map(shards, mesh=mesh, in_specs=in_specs, out_specs=out_specs, check_vma=False)
```

```python
import jax
import jax.numpy as jnp
from jax import lax
from jax.experimental import pallas as pl
from jax.experimental.pallas import tpu as pltpu
from jax.sharding import PartitionSpec as P

COLS = 32
BLOCKS = 64
DOF = 384
MODES = 36
SLOTS = 8
PAIRS = 128
AGG = 4
LANES = 128
PAIRED = 3
STRIDE = 64
WIDTH = AGG * STRIDE

fine_damping = 0.6
coarse_damping = 0.7
f32 = jnp.float32
bf16 = jnp.bfloat16

NN = (((1,), (0,)), ((), ()))
NT = (((1,), (1,)), ((), ()))


def dot(a, b, dims=NN):
    return lax.dot_general(a, b, dims, preferred_element_type=f32)


def split2(x):
    hi = x.astype(bf16)
    lo = (x - hi.astype(f32)).astype(bf16)
    return hi, lo


def split3(x):
    hi = x.astype(bf16)
    rest = x - hi.astype(f32)
    mid = rest.astype(bf16)
    lo = (rest - mid.astype(f32)).astype(bf16)
    return hi, mid, lo


def mm3(x, whi, wlo, dims=NN):
    rows = x.shape[0]
    hi, lo = split2(x)
    first = dot(jnp.concatenate([hi, lo], axis=0), whi, dims)
    return first[:rows] + first[rows:] + dot(hi, wlo, dims)


def mm2(x, w, dims=NN):
    rows = x.shape[0]
    hi, lo = split2(x)
    both = dot(jnp.concatenate([hi, lo], axis=0), w, dims)
    return both[:rows] + both[rows:]


def mm_exact(x, w, dims=NN):
    rows = x.shape[0]
    parts = dot(jnp.concatenate(split3(x), axis=0), w, dims)
    return parts[:rows] + parts[rows : 2 * rows] + parts[2 * rows :]


def iota(shape, axis):
    return lax.broadcasted_iota(jnp.int32, shape, axis)


def permutation():
    i = iota((DOF, DOF), 0)
    j = iota((DOF, DOF), 1)
    return (i == 6 * (j & 63) + (j >> 6)).astype(f32).astype(bf16)


def permutation_back():
    i = iota((DOF, DOF), 0)
    j = iota((DOF, DOF), 1)
    return (j == 6 * (i & 63) + (i >> 6)).astype(f32).astype(bf16)


def hot_twice(index):
    k = iota((LANES, PAIRS), 0) & 63
    return (k == index.astype(jnp.int32)).astype(f32).astype(bf16)


def hot_paired(index):
    r = iota((LANES, 2 * PAIRS), 0)
    doubled = jnp.concatenate([index.astype(jnp.int32)] * 2, axis=1)
    want = doubled + 64 * (iota((1, 2 * PAIRS), 1) >> 7)
    return (r == want).astype(f32).astype(bf16)


def wide(t):
    return jnp.concatenate([t] * PAIRED, axis=1)


def stack_fields(v):
    rows = []
    for m in range(PAIRED):
        rows.append(jnp.concatenate([x[:, m * LANES : (m + 1) * LANES] for x in v], axis=1))
    return jnp.concatenate(rows, axis=0)


def unstack_fields(y, count):
    out = []
    for a in range(count):
        parts = [
            y[m * COLS : (m + 1) * COLS, a * LANES : (a + 1) * LANES] for m in range(PAIRED)
        ]
        out.append(jnp.concatenate(parts, axis=1))
    return out


def rows_of(x):
    return jnp.concatenate([x[:, m * LANES : (m + 1) * LANES] for m in range(PAIRED)], axis=0)


def lanes_of(x):
    r = x.shape[0] // PAIRED
    return jnp.concatenate([x[m * r : (m + 1) * r] for m in range(PAIRED)], axis=1)


def local_product(v, khi, klo, ghi, glo, cross):
    springs = unstack_fields(mm3(stack_fields(v), ghi, glo), AGG)
    return [
        mm3(v[a], khi[a], klo[a]) + (springs[a] + v[a] * cross[a]) for a in range(AGG)
    ]


def to_own(vh, xhi, xlo):
    return lanes_of(mm3(rows_of(vh), xhi, xlo, NT))


def to_halo(v, xhi, xlo):
    return lanes_of(mm3(rows_of(v), xhi, xlo))


def pick(flag, a, b):
    return jnp.where(flag, a, b)


def send(parity, message, blk1, blk0, band1, band0):
    odd_s = parity[0] == 1
    odd_b = parity[1] == 1
    blk1[...] = pick(odd_s, message[2], message[0])
    blk0[...] = pick(odd_s, message[0], message[2])
    band1[...] = pick(odd_b, message[3], message[1])
    band0[...] = pick(odd_b, message[1], message[3])


def receive(parity, blk1, blk0, band1, band0):
    odd_s = parity[0] == 1
    odd_b = parity[1] == 1
    blk1, blk0, band1, band0 = blk1[...], blk0[...], band1[...], band0[...]
    return [
        pick(odd_s, blk0, blk1),
        pick(odd_b, band0, band1),
        pick(odd_s, blk1, blk0),
        pick(odd_b, band1, band0),
    ]


def block_diagonal(blocks):
    rows = []
    for j in range(AGG):
        parts = []
        if j > 0:
            parts.append(jnp.zeros((STRIDE, j * STRIDE), f32))
        parts.append(blocks[j])
        if j < AGG - 1:
            parts.append(jnp.zeros((STRIDE, (AGG - 1 - j) * STRIDE), f32))
        rows.append(jnp.concatenate(parts, axis=1))
    return jnp.concatenate(rows, axis=0)


def store2(hi_ref, lo_ref, x):
    hi, lo = split2(x)
    hi_ref[...] = hi
    lo_ref[...] = lo


def sent_modes(sent):
    pad = jnp.zeros((STRIDE - MODES, DOF), f32)
    return jnp.concatenate([sent[32:68], pad], axis=0).astype(bf16)


def sent_diagonal(sent):
    tail = sent[72:80]
    return jnp.concatenate([tail[:, t * STRIDE : (t + 1) * STRIDE] for t in range(5)], axis=0)


def with_modes(field, part):
    side = [part[8 * t : 8 * t + 8] for t in range(4)] + [jnp.zeros((8, LANES), f32)]
    return jnp.concatenate([field, jnp.concatenate(side, axis=1)], axis=0)


def modes_below(sent):
    tail = sent[COLS : COLS + 8]
    return jnp.concatenate([tail[:, t * STRIDE : (t + 1) * STRIDE] for t in range(4)], axis=0)


def pair_weights(own, far, w, xhi, xlo, j):
    w3 = jnp.concatenate(split3(w), axis=0)
    total = wide(jnp.sum(dot(w3, hot_twice(own), NT), axis=0, keepdims=True))
    total_far = wide(jnp.sum(dot(w3, hot_twice(far), NT), axis=0, keepdims=True))
    near = hot_paired(own)
    hi, mid, lo = split3(jnp.concatenate([w, w], axis=1))
    m = dot(jnp.concatenate([near * hi, near * mid, near * lo], axis=0), hot_paired(far), NT)
    m = m[0:LANES] + m[LANES : 2 * LANES] + m[2 * LANES :]
    hi, lo = split2(m)
    xhi[j] = hi
    xlo[j] = lo
    return total, total_far


def first_kernel(
    parity, b_in, k_in, q_in, nb_in, valid_in, left_in, right_in, penalty_in,
    blk1, blk0, band1, band0, tab,
    b, k, q, nb, valid, left, right, penalty, sem,
):
    small = [
        pltpu.make_async_copy(src, dst, sem.at[n])
        for n, (src, dst) in enumerate(
            [
                (nb_in, nb),
                (valid_in, valid),
                (left_in, left),
                (right_in, right),
                (penalty_in, penalty),
                (q_in, q),
                (b_in, b),
            ]
        )
    ]
    large = [pltpu.make_async_copy(k_in.at[a], k.at[a], sem.at[8 + a]) for a in range(AGG)]
    for copy in small + large:
        copy.start()
    perm = permutation()
    expand = (iota((SLOTS, PAIRS), 0) == (iota((SLOTS, PAIRS), 1) >> 4)).astype(f32).astype(bf16)
    for copy in small:
        copy.wait()

    listed = jnp.concatenate([nb[...], valid[...]], axis=0).astype(f32).astype(bf16)
    listed = dot(listed, expand)
    slot = listed[0:AGG]
    weight = penalty[...] * listed[AGG:]
    crossing = slot > 3.5
    lf = left[...].astype(f32)
    rf = right[...].astype(f32)
    far = slot * 64.0 + rf
    wloc = jnp.where(crossing, 0.0, weight)
    wcross = jnp.where(crossing, weight, 0.0)
    tab[0:4] = lf
    tab[4:8] = rf
    tab[8:12] = far
    tab[12:16] = wloc
    tab[16:20] = wcross

    rr = iota((AGG * LANES, PAIRS), 0)
    row = (rr >> 7) * 64 + (rr & 63)
    lefts = lf.astype(jnp.int32)
    fars = far.astype(jnp.int32)
    hits = []
    for a in range(AGG):
        near = jnp.where(row == lefts[a : a + 1] + a * BLOCKS, 1.0, 0.0)
        hits.append((near + jnp.where(row == fars[a : a + 1], 1.0, 0.0)).astype(bf16))
    flat = jnp.concatenate([wloc[a : a + 1] for a in range(AGG)], axis=1)
    total = dot(jnp.concatenate(split3(flat), axis=0), jnp.concatenate(hits, axis=1), NT)
    total = jnp.sum(total, axis=0, keepdims=True)
    totals = []
    for a in range(AGG):
        tab[20 + a : 21 + a] = total[:, a * LANES : (a + 1) * LANES]
        totals.append(wide(total[:, a * LANES : (a + 1) * LANES]))

    pad = jnp.zeros((STRIDE - MODES, DOF), f32)
    q_all = q[...].astype(f32)
    modes = [jnp.concatenate([q_all[:, a, :], pad], axis=0).astype(bf16) for a in range(AGG)]
    turned_modes = dot(jnp.concatenate(modes, axis=0), perm)
    turned_modes = [turned_modes[a * STRIDE : (a + 1) * STRIDE] for a in range(AGG)]
    turned = mm_exact(jnp.concatenate([b[a] for a in range(AGG)], axis=0), perm)
    eye = iota((LANES, LANES), 0) == iota((LANES, LANES), 1)
    turned16 = [turned_modes[a].astype(bf16) for a in range(AGG)]
    springs = [mm2(turned_modes[a] * totals[a], turned16[a], NT) for a in range(AGG)]
    diagonals, wholes = [], []
    for copy in large:
        copy.wait()
    for a in range(AGG):
        cuts = []
        for m in range(PAIRED):
            tile = k[a, m * LANES : (m + 1) * LANES, m * LANES : (m + 1) * LANES]
            cuts.append(jnp.sum(jnp.where(eye, tile, 0.0), axis=0, keepdims=True))
        diagonals.append(jnp.concatenate(cuts, axis=1))
        hi, lo = split2(k[a])
        projected = dot(modes[a], hi) + dot(modes[a], lo)
        wholes.append(mm2(projected, modes[a], NT) + springs[a])
    diagonals = mm_exact(jnp.concatenate(diagonals + [jnp.zeros((4, DOF), f32)], axis=0), perm)
    messages = []
    for a in range(AGG):
        load = turned[a * COLS : (a + 1) * COLS]
        diagonal = diagonals[a : a + 1] + totals[a]
        whole = wholes[a]
        table = jnp.concatenate([lf[a : a + 1], rf[a : a + 1], wcross[a : a + 1]], axis=1)
        side = [whole[8 * t : 8 * t + 8] for t in range(5)] + [jnp.zeros((8, STRIDE), f32)]
        messages.append(
            jnp.concatenate(
                [
                    load,
                    turned_modes[a][0:32],
                    jnp.concatenate([turned_modes[a][32:36], diagonal, table], axis=0),
                    jnp.zeros((2, DOF), f32),
                    jnp.concatenate(side, axis=1),
                ],
                axis=0,
            )
        )
    send(parity, messages, blk1, blk0, band1, band0)


def local_kernel(
    parity, blk1, blk0, band1, band0, tab, k_in,
    pkhi, pklo, ghi, glo, aqhi, aqlo, big, xhi, xlo, tco, tch, bp, qp, dsum, dloc, work, k, sem,
):
    copies = [
        pltpu.make_async_copy(
            k_in.at[a, :, pl.ds(m * LANES, LANES)], k.at[a, m], sem.at[a * PAIRED + m]
        )
        for a in range(AGG)
        for m in range(PAIRED)
    ]
    for copy in copies:
        copy.start()
    for a, sent in enumerate(receive(parity, blk1, blk0, band1, band0)):
        bp[a] = sent[0:COLS]
        qp[a] = sent_modes(sent)
        dsum[a] = sent_diagonal(sent)
        dloc[a : a + 1] = sent[68:69]
    perm = permutation()
    for a in range(AGG):
        tiles = []
        for m in range(PAIRED):
            copies[a * PAIRED + m].wait()
            picked = [k[a, m, pl.ds(c, BLOCKS, stride=6), :] for c in range(6)]
            tiles.append(jnp.concatenate(picked, axis=0))
        hi, lo = split2(jnp.concatenate(tiles, axis=1))
        both = dot(jnp.concatenate([hi, lo], axis=0), perm).astype(bf16)
        pkhi[a] = both[0:DOF]
        pklo[a] = both[DOF:]
    r = iota((AGG * LANES, 2 * PAIRS), 0)
    shift = 64 * (iota((1, 2 * PAIRS), 1) >> 7)
    rows = []
    for a in range(AGG):
        fi = tab[8 + a : 9 + a].astype(jnp.int32)
        fi = (fi >> 6) * LANES + (fi & 63)
        f2 = jnp.concatenate([fi] * 2, axis=1) + shift
        w2 = jnp.concatenate([tab[12 + a : 13 + a]] * 2, axis=1)
        far = (r == f2).astype(f32).astype(bf16)
        hi, mid, lo = split3(w2)
        near = hot_paired(tab[a : a + 1])
        parts = jnp.concatenate([near * hi, near * mid, near * lo], axis=0)
        m = dot(parts, far, NT)
        rows.append(m[0:LANES] + m[LANES : 2 * LANES] + m[2 * LANES :])
    mm = jnp.concatenate(rows, axis=0)
    work[...] = mm + mm.T
    eye = iota((AGG * LANES, AGG * LANES), 0) == iota((AGG * LANES, AGG * LANES), 1)
    total = jnp.concatenate([tab[20 + a : 21 + a] for a in range(AGG)], axis=1)
    gh, gl = split2(jnp.where(eye, total, 0.0) - work[...])
    ghi[...] = gh
    glo[...] = gl
    lines = []
    for a in range(AGG):
        rows = rows_of(qp[a].astype(f32)).astype(bf16)
        y = dot(rows, gh[a * LANES : (a + 1) * LANES]) + dot(rows, gl[a * LANES : (a + 1) * LANES])
        turned = dot(qp[a], pkhi[a]) + dot(qp[a], pklo[a])
        parts = []
        for c in range(AGG):
            part = lanes_of(y[:, c * LANES : (c + 1) * LANES])
            parts.append(part + turned if c == a else part)
        lines.append(jnp.concatenate(parts, axis=1))
    aq = jnp.concatenate(lines, axis=0)
    ah, al = split2(aq)
    aqhi[...] = ah
    aqlo[...] = al
    columns = []
    for a in range(AGG):
        both = jnp.concatenate([ah, al], axis=0)[:, a * DOF : (a + 1) * DOF]
        block = dot(both, qp[a], NT)
        columns.append(block[:WIDTH] + block[WIDTH:])
    big[...] = jnp.concatenate(columns, axis=1)
    for j in range(2, AGG):
        tco[j : j + 1], tch[j : j + 1] = pair_weights(
            tab[j : j + 1], tab[4 + j : 5 + j], tab[16 + j : 17 + j], xhi, xlo, j - 2
        )
    tco[0:2] = jnp.zeros((2, DOF), f32)
    tch[0:2] = jnp.zeros((2, DOF), f32)


def second_kernel(
    parity, blk1, blk0, band1, band0, bp, qp, dloc, khi, klo, ghi, glo, aqhi, aqlo, x2hi, x2lo, t2o, t2h,
    oblk1, oblk0, oband1, oband0, xhi, xlo, rec, rech, qh, cdh, tco, tch, x2o, r1o, dlt, pgo,
):
    halo = receive(parity, blk1, blk0, band1, band0)
    cross, xs, xh = [], [], []
    for j in range(AGG):
        if j < 2:
            table = halo[j][69:70]
            total, total_far = pair_weights(
                table[:, PAIRS : 2 * PAIRS], table[:, 0:PAIRS], table[:, 2 * PAIRS :], xhi, xlo, j
            )
        else:
            xhi[j] = x2hi[j - 2]
            xlo[j] = x2lo[j - 2]
            total, total_far = t2o[j : j + 1], t2h[j : j + 1]
        cross.append(total)
        tco[j : j + 1] = total
        tch[j : j + 1] = total_far
        inverse = fine_damping / (dloc[j : j + 1] + total)
        inverseh = fine_damping / (halo[j][68:69] + total_far)
        rec[j : j + 1] = inverse
        rech[j : j + 1] = inverseh
        qh[j] = sent_modes(halo[j])
        cdh[j] = sent_diagonal(halo[j])
        xs.append(inverse * bp[j])
        xh.append(inverseh * halo[j][0:COLS])
    kh = [khi[a] for a in range(AGG)]
    kl = [klo[a] for a in range(AGG)]
    y = local_product(xs, kh, kl, ghi[...], glo[...], cross)
    d, pg = [], []
    for j in range(AGG):
        r1 = bp[j] - y[j] + to_own(xh[j], xhi[j], xlo[j])
        step = rec[j : j + 1] * r1
        d.append(step)
        dlt[j] = step
        x2o[j] = xs[j] + step
        r1o[j] = r1
        pg.append(mm2(r1 - step * cross[j], qp[j], NT))
    pg = jnp.concatenate(pg, axis=1) - mm3(jnp.concatenate(d, axis=1), aqhi[...], aqlo[...], NT)
    pgo[...] = pg
    messages = []
    for j in range(AGG):
        part = pg[:, j * STRIDE : (j + 1) * STRIDE]
        messages.append(with_modes(d[j], part))
    send(parity, messages, oblk1, oblk0, oband1, oband0)


def inverse_kernel(
    dlt, r1, khi, klo, ghi, glo, qp, qh, dsum, cdh, tco, tch, xhi, xlo, big,
    pr, yhi, ylo, zhi, zlo, ghp, hhi, hlo, hhhi, hhlo, gchi, gclo, gxhi, gxlo, gohi, golo, work,
):
    d = [dlt[j] for j in range(AGG)]
    corner, couple, part = [], [], []
    for j in range(AGG):
        mine = qp[j].astype(f32)
        other = qh[j].astype(f32)
        own = mm2(mine * tco[j : j + 1], qp[j], NT)
        corner.append(own)
        blank = jnp.zeros((MODES, LANES - STRIDE), f32)
        work[:, j, :] = jnp.concatenate([dsum[j][0:MODES] + own[0:MODES], blank], axis=1)
        far = mm2(other * tch[j : j + 1], qh[j], NT)
        work[:, AGG + j, :] = jnp.concatenate([cdh[j][0:MODES] + far[0:MODES], blank], axis=1)

    def own_side(j):
        rows = rows_of(qp[j].astype(f32)).astype(bf16)
        y = lanes_of(dot(rows, xhi[j]) + dot(rows, xlo[j]))
        hi, lo = split2(y)
        yhi[j] = hi
        ylo[j] = lo
        couple.append(-(dot(hi, qh[j], NT) + dot(lo, qh[j], NT)))

    def far_side(j):
        rows = rows_of(qh[j].astype(f32)).astype(bf16)
        z = lanes_of(dot(rows, xhi[j], NT) + dot(rows, xlo[j], NT))
        hi, lo = split2(z)
        zhi[j] = hi
        zlo[j] = lo
        part.append(mm3(d[j], hi, lo, NT))

    springs = []

    def spring_side(j):
        if j == 0:
            springs.extend(unstack_fields(mm3(stack_fields(d), ghi[...], glo[...]), AGG))

    def bend_side(j):
        bend = mm3(d[j], khi[j], klo[j])
        pr[j] = r1[j] - (bend + (springs[j] + d[j] * tco[j : j + 1]))

    tasks = [(f, j) for f in (own_side, far_side, spring_side, bend_side) for j in range(AGG)]
    lane = iota((8, LANES), 1)
    rows = [work[i] + jnp.where(lane == STRIDE + i, 1.0, 0.0) for i in range(MODES)]

    def column(i, s):
        return jnp.broadcast_to(rows[i][:, s : s + 1], (8, LANES))

    for s in range(0, MODES, 2):
        p, q = s, s + 1
        pp, pq, qq, qp_ = column(p, p), column(p, q), column(q, q), column(q, p)
        scale = 1.0 / (pp * qq - pq * qp_)
        first = (qq * scale) * rows[p] - (pq * scale) * rows[q]
        second = (pp * scale) * rows[q] - (qp_ * scale) * rows[p]
        for i in range(MODES):
            if i != p and i != q:
                rows[i] = rows[i] - column(i, p) * first - column(i, q) * second
        rows[p], rows[q] = first, second
        if tasks:
            task, at = tasks.pop(0)
            task(at)
    for task, at in tasks:
        task(at)
    ghp[...] = jnp.concatenate(part, axis=1)
    for i in range(MODES):
        work[i] = rows[i] * coarse_damping
    below = jnp.zeros((STRIDE - MODES, STRIDE), f32)
    blocks = [
        jnp.concatenate([work[:, m, :][:, STRIDE:], below], axis=0) for m in range(2 * AGG)
    ]
    hh, hl = split2(block_diagonal(blocks[:AGG]))
    hhi[...] = hh
    hlo[...] = hl
    fh, fl = split2(block_diagonal(blocks[AGG:]))
    hhhi[...] = fh
    hhlo[...] = fl
    eye = iota((WIDTH, WIDTH), 0) == iota((WIDTH, WIDTH), 1)
    whole = big[...] + block_diagonal(corner)
    store2(gchi, gclo, jnp.where(eye, 1.0, 0.0) - mm3(whole, hh, hl))
    store2(gxhi, gxlo, -mm3(block_diagonal([c.T for c in couple]), hh, hl))
    store2(gohi, golo, -mm3(block_diagonal(couple), fh, fl))


def halo_modes(halo, at):
    return jnp.concatenate([h[:, at : at + STRIDE] for h in halo], axis=1)


def third_kernel(
    parity, blk1, blk0, band1, band0, pg, ghp, yhi, ylo, hhi, hlo, hhhi, hhlo, gchi, gclo, gxhi, gxlo,
    oblk1, oblk0, oband1, oband0, e1o, d1o, p2o, dh,
):
    halo = receive(parity, blk1, blk0, band1, band0)
    parts = []
    for j in range(AGG):
        value = halo[j][0:COLS]
        dh[j] = value
        parts.append(mm3(value, yhi[j], ylo[j], NT))
    g = pg[...] + jnp.concatenate(parts, axis=1)
    gh = jnp.concatenate([modes_below(h) for h in halo], axis=1) + ghp[...]
    e0 = mm3(g, hhi[...], hlo[...])
    e0h = mm3(gh, hhhi[...], hhlo[...])
    gch, gcl = gchi[...], gclo[...]
    d1 = mm3(e0, gch, gcl) + mm3(e0h, gxhi[...], gxlo[...])
    p2 = mm3(d1, gch, gcl)
    e1o[...] = e0 + d1
    d1o[...] = d1
    p2o[...] = p2
    messages = []
    for j in range(AGG):
        cut = slice(j * STRIDE, (j + 1) * STRIDE)
        messages.append(jnp.concatenate([d1[:, cut], p2[:, cut]], axis=1))
    send(parity, messages, oblk1, oblk0, oband1, oband0)


def beside_third_kernel(dh, pr, xhi, xlo, d1, gohi, golo, r2o, w2o):
    w2o[...] = mm3(d1[...], gohi[...], golo[...])
    for j in range(AGG):
        r2o[j] = pr[j] + to_own(dh[j], xhi[j], xlo[j])


def fourth_kernel(
    parity, blk1, blk0, band1, band0, p2, w2, e1, gchi, gclo, gxhi, gxlo, r2, qp, aqhi, aqlo, tco,
    oblk1, oblk0, oband1, oband0, eo, f3o, pr3o,
):
    halo = receive(parity, blk1, blk0, band1, band0)
    gxh, gxl = gxhi[...], gxlo[...]
    d2 = p2[...] + mm3(halo_modes(halo, 0), gxh, gxl)
    d2h = halo_modes(halo, STRIDE) + w2[...]
    d3 = mm3(d2, gchi[...], gclo[...]) + mm3(d2h, gxh, gxl)
    e = e1[...] + d2 + d3
    eo[...] = e
    y = mm3(e, aqhi[...], aqlo[...])
    messages = []
    for j in range(AGG):
        mine = e[:, j * STRIDE : (j + 1) * STRIDE]
        f = mm2(mine, qp[j])
        f3o[j] = f
        part = r2[j] - y[:, j * DOF : (j + 1) * DOF] - f * tco[j : j + 1]
        pr3o[j] = part
        messages.append(with_modes(part, mine))
    send(parity, messages, oblk1, oblk0, oband1, oband0)


def beside_fourth_kernel(e, x2, f3, yhi, ylo, x3o, rho):
    for j in range(AGG):
        x3o[j] = x2[j] + f3[j]
        rho[j] = mm3(e[:, j * STRIDE : (j + 1) * STRIDE], yhi[j], ylo[j])


def last_kernel(
    parity, blk1, blk0, band1, band0, x3, pr3, rh3, zhi, zlo, rec, rech, khi, klo, ghi, glo, tco, xhi, xlo,
    field, residual,
):
    halo = receive(parity, blk1, blk0, band1, band0)
    d4, d4h, r3 = [], [], []
    for j in range(AGG):
        r = pr3[j] + mm3(modes_below(halo[j]), zhi[j], zlo[j])
        rh = halo[j][0:COLS] + rh3[j]
        r3.append(r)
        d4.append(rec[j : j + 1] * r)
        d4h.append(rech[j : j + 1] * rh)
    cross = [tco[j : j + 1] for j in range(AGG)]
    y = local_product(
        d4, [khi[a] for a in range(AGG)], [klo[a] for a in range(AGG)], ghi[...], glo[...], cross
    )
    out = []
    for j in range(AGG):
        out.append(x3[j] + d4[j])
    for j in range(AGG):
        out.append(r3[j] - y[j] + to_own(d4h[j], xhi[j], xlo[j]))
    turned = mm_exact(jnp.concatenate(out, axis=0), permutation_back())
    for j in range(AGG):
        field[j] = turned[j * COLS : (j + 1) * COLS]
        residual[j] = turned[(AGG + j) * COLS : (AGG + j + 1) * COLS]


VM = pl.BlockSpec(memory_space=pltpu.VMEM)
SM = pl.BlockSpec(memory_space=pltpu.SMEM)
HB = pl.BlockSpec(memory_space=pltpu.HBM)


def run(kernel, outs, *args, scalars=0, far=0, scratch=()):
    near = len(args) - far
    args = args[:near] + tuple(
        pltpu.with_memory_space_constraint(x, pltpu.HBM) for x in args[near:]
    )
    return pl.pallas_call(
        kernel,
        out_shape=[jax.ShapeDtypeStruct(shape, kind) for shape, kind in outs],
        in_specs=[SM] * scalars + [VM] * (near - scalars) + [HB] * far,
        out_specs=[VM] * len(outs),
        scratch_shapes=list(scratch),
        compiler_params=pltpu.CompilerParams(vmem_limit_bytes=24 * 2**20),
    )(*args)


def swapped(x, axis, odd):
    length = lax.axis_size(axis)
    route = []
    for i in range(odd, length + odd, 2):
        near, far = i % length, (i + 1) % length
        route += [(near, far), (far, near)]
    return lax.ppermute(x, axis, route)


def exchange(messages):
    blk1, blk0, band1, band0 = messages
    in0 = swapped(band0, "band", 0)
    in1 = swapped(band1, "band", 1)
    in2 = swapped(blk0, "blk", 0)
    in3 = swapped(blk1, "blk", 1)
    return in3, in2, in1, in0


def shards(
    load_columns, stiffness, rigid_modes, neighbours, slot_valid, pair_left, pair_right, penalty
):
    parity = jnp.stack([lax.axis_index("blk") % 2, lax.axis_index("band") % 2]).astype(jnp.int32)
    fields = ((AGG, COLS, DOF), f32)
    modes = ((AGG, STRIDE, DOF), bf16)
    square = ((AGG, DOF, DOF), bf16)
    local = ((AGG * LANES, AGG * LANES), bf16)
    small = ((AGG, 40, STRIDE), f32)
    tile = ((AGG, LANES, LANES), bf16)
    rows = ((AGG, DOF), f32)
    coarse = ((COLS, WIDTH), f32)
    broad = ((WIDTH, AGG * DOF), bf16)
    dense = ((WIDTH, WIDTH), bf16)

    def message(height, width):
        return [((height, width), f32)] * 4

    *out, tab = run(
        first_kernel,
        message(80, DOF) + [((24, PAIRS), f32)],
        parity,
        load_columns[0, 0],
        stiffness[0, 0],
        jnp.transpose(rigid_modes[0, 0], (1, 0, 2)),
        neighbours[0, 0],
        slot_valid[0, 0],
        pair_left[0, 0],
        pair_right[0, 0],
        penalty[0, 0],
        scalars=1,
        far=8,
        scratch=[
            pltpu.VMEM((AGG, COLS, DOF), f32),
            pltpu.VMEM((AGG, DOF, DOF), f32),
            pltpu.VMEM((MODES, AGG, DOF), bf16),
            pltpu.VMEM((AGG, SLOTS), jnp.int32),
            pltpu.VMEM((AGG, SLOTS), jnp.int32),
            pltpu.VMEM((AGG, PAIRS), jnp.int32),
            pltpu.VMEM((AGG, PAIRS), jnp.int32),
            pltpu.VMEM((AGG, PAIRS), f32),
            pltpu.SemaphoreType.DMA((12,)),
        ],
    )
    got = exchange(out)
    pair_tile = ((2, LANES, LANES), bf16)
    pkhi, pklo, ghi, glo, aqhi, aqlo, big, x2hi, x2lo, t2o, t2h, bp, qp, dsum, dloc = run(
        local_kernel,
        [square, square, local, local, broad, broad, ((WIDTH, WIDTH), f32), pair_tile, pair_tile, rows, rows]
        + [fields, modes, small, rows],
        parity, *out, tab, stiffness[0, 0],
        scalars=1,
        far=1,
        scratch=[
            pltpu.VMEM((AGG * LANES, AGG * LANES), f32),
            pltpu.VMEM((AGG, PAIRED, DOF, LANES), f32),
            pltpu.SemaphoreType.DMA((AGG * PAIRED,)),
        ],
    )
    *out, xhi, xlo, rec, rech, qh, cdh, tco, tch, x2, r1, dlt, pg = run(
        second_kernel,
        message(COLS + 8, DOF)
        + [tile, tile, rows, rows, modes, small, rows, rows, fields, fields, fields, coarse],
        parity, *got, bp, qp, dloc, pkhi, pklo, ghi, glo, aqhi, aqlo, x2hi, x2lo, t2o, t2h,
        scalars=1,
    )
    got = exchange(out)
    pr, yhi, ylo, zhi, zlo, ghp, hhi, hlo, hhhi, hhlo, gchi, gclo, gxhi, gxlo, gohi, golo = run(
        inverse_kernel,
        [fields, modes, modes, modes, modes, coarse] + [dense] * 10,
        dlt, r1, pkhi, pklo, ghi, glo, qp, qh, dsum, cdh, tco, tch, xhi, xlo, big,
        scratch=[pltpu.VMEM((MODES, 2 * AGG, LANES), f32)],
    )
    *out, e1, d1, p2, dh = run(
        third_kernel,
        message(COLS, LANES) + [coarse, coarse, coarse, fields],
        parity, *got, pg, ghp, yhi, ylo, hhi, hlo, hhhi, hhlo, gchi, gclo, gxhi, gxlo,
        scalars=1,
    )
    got = exchange(out)
    r2, w2 = run(beside_third_kernel, [fields, coarse], dh, pr, xhi, xlo, d1, gohi, golo)
    *out, e, f3, pr3 = run(
        fourth_kernel,
        message(COLS + 8, DOF) + [coarse, fields, fields],
        parity, *got, p2, w2, e1, gchi, gclo, gxhi, gxlo, r2, qp, aqhi, aqlo, tco,
        scalars=1,
    )
    got = exchange(out)
    x3, rh3 = run(beside_fourth_kernel, [fields, fields], e, x2, f3, yhi, ylo)
    field, residual = run(
        last_kernel,
        [fields, fields],
        parity, *got, x3, pr3, rh3, zhi, zlo, rec, rech, pkhi, pklo, ghi, glo, tco, xhi, xlo,
        scalars=1,
    )
    return (field[None, None], residual[None, None])


def solution(mesh):
    in_specs = (
        P("band", "blk", None, None, None),
        P("band", "blk", None, None, None),
        P("band", "blk", None, None, None),
        P("band", "blk", None, None),
        P("band", "blk", None, None),
        P("band", "blk", None, None),
        P("band", "blk", None, None),
        P("band", "blk", None, None),
    )
    out_specs = (P("band", "blk", None, None, None), P("band", "blk", None, None, None))
    return jax.shard_map(shards, mesh=mesh, in_specs=in_specs, out_specs=out_specs, check_vma=False)
```

```python
import jax
import jax.numpy as jnp
from jax import lax
from jax.experimental import pallas as pl
from jax.experimental.pallas import tpu as pltpu
from jax.sharding import PartitionSpec as P

COLS = 32
BLOCKS = 64
DOF = 384
MODES = 36
SLOTS = 8
PAIRS = 128
AGG = 4
LANES = 128
PAIRED = 3
STRIDE = 64
WIDTH = AGG * STRIDE

fine_damping = 0.6
coarse_damping = 0.7
f32 = jnp.float32
bf16 = jnp.bfloat16

NN = (((1,), (0,)), ((), ()))
NT = (((1,), (1,)), ((), ()))


def dot(a, b, dims=NN):
    return lax.dot_general(a, b, dims, preferred_element_type=f32)


def split2(x):
    hi = x.astype(bf16)
    lo = (x - hi.astype(f32)).astype(bf16)
    return hi, lo


def split3(x):
    hi = x.astype(bf16)
    rest = x - hi.astype(f32)
    mid = rest.astype(bf16)
    lo = (rest - mid.astype(f32)).astype(bf16)
    return hi, mid, lo


def mm3(x, whi, wlo, dims=NN):
    rows = x.shape[0]
    hi, lo = split2(x)
    first = dot(jnp.concatenate([hi, lo], axis=0), whi, dims)
    return first[:rows] + first[rows:] + dot(hi, wlo, dims)


def mm2(x, w, dims=NN):
    rows = x.shape[0]
    hi, lo = split2(x)
    both = dot(jnp.concatenate([hi, lo], axis=0), w, dims)
    return both[:rows] + both[rows:]


def mm_exact(x, w, dims=NN):
    rows = x.shape[0]
    parts = dot(jnp.concatenate(split3(x), axis=0), w, dims)
    return parts[:rows] + parts[rows : 2 * rows] + parts[2 * rows :]


def iota(shape, axis):
    return lax.broadcasted_iota(jnp.int32, shape, axis)


def permutation():
    i = iota((DOF, DOF), 0)
    j = iota((DOF, DOF), 1)
    return (i == 6 * (j & 63) + (j >> 6)).astype(f32).astype(bf16)


def permutation_back():
    i = iota((DOF, DOF), 0)
    j = iota((DOF, DOF), 1)
    return (j == 6 * (i & 63) + (i >> 6)).astype(f32).astype(bf16)


def hot_twice(index):
    k = iota((LANES, PAIRS), 0) & 63
    return (k == index.astype(jnp.int32)).astype(f32).astype(bf16)


def hot_paired(index):
    r = iota((LANES, 2 * PAIRS), 0)
    doubled = jnp.concatenate([index.astype(jnp.int32)] * 2, axis=1)
    want = doubled + 64 * (iota((1, 2 * PAIRS), 1) >> 7)
    return (r == want).astype(f32).astype(bf16)


def wide(t):
    return jnp.concatenate([t] * PAIRED, axis=1)


def stack_fields(v):
    rows = []
    for m in range(PAIRED):
        rows.append(jnp.concatenate([x[:, m * LANES : (m + 1) * LANES] for x in v], axis=1))
    return jnp.concatenate(rows, axis=0)


def unstack_fields(y, count):
    out = []
    for a in range(count):
        parts = [
            y[m * COLS : (m + 1) * COLS, a * LANES : (a + 1) * LANES] for m in range(PAIRED)
        ]
        out.append(jnp.concatenate(parts, axis=1))
    return out


def rows_of(x):
    return jnp.concatenate([x[:, m * LANES : (m + 1) * LANES] for m in range(PAIRED)], axis=0)


def lanes_of(x):
    r = x.shape[0] // PAIRED
    return jnp.concatenate([x[m * r : (m + 1) * r] for m in range(PAIRED)], axis=1)


def local_product(v, khi, klo, ghi, glo, cross):
    springs = unstack_fields(mm3(stack_fields(v), ghi, glo), AGG)
    return [
        mm3(v[a], khi[a], klo[a]) + (springs[a] + v[a] * cross[a]) for a in range(AGG)
    ]


def to_own(vh, xhi, xlo):
    return lanes_of(mm3(rows_of(vh), xhi, xlo, NT))


def to_halo(v, xhi, xlo):
    return lanes_of(mm3(rows_of(v), xhi, xlo))


def pick(flag, a, b):
    return jnp.where(flag, a, b)


def send(parity, message, blk1, blk0, band1, band0):
    odd_s = parity[0] == 1
    odd_b = parity[1] == 1
    blk1[...] = pick(odd_s, message[2], message[0])
    blk0[...] = pick(odd_s, message[0], message[2])
    band1[...] = pick(odd_b, message[3], message[1])
    band0[...] = pick(odd_b, message[1], message[3])


def receive(parity, blk1, blk0, band1, band0):
    odd_s = parity[0] == 1
    odd_b = parity[1] == 1
    blk1, blk0, band1, band0 = blk1[...], blk0[...], band1[...], band0[...]
    return [
        pick(odd_s, blk0, blk1),
        pick(odd_b, band0, band1),
        pick(odd_s, blk1, blk0),
        pick(odd_b, band1, band0),
    ]


def block_diagonal(blocks):
    rows = []
    for j in range(AGG):
        parts = []
        if j > 0:
            parts.append(jnp.zeros((STRIDE, j * STRIDE), f32))
        parts.append(blocks[j])
        if j < AGG - 1:
            parts.append(jnp.zeros((STRIDE, (AGG - 1 - j) * STRIDE), f32))
        rows.append(jnp.concatenate(parts, axis=1))
    return jnp.concatenate(rows, axis=0)


def store2(hi_ref, lo_ref, x):
    hi, lo = split2(x)
    hi_ref[...] = hi
    lo_ref[...] = lo


def sent_modes(sent):
    pad = jnp.zeros((STRIDE - MODES, DOF), f32)
    return jnp.concatenate([sent[32:68], pad], axis=0).astype(bf16)


def sent_diagonal(sent):
    tail = sent[72:80]
    return jnp.concatenate([tail[:, t * STRIDE : (t + 1) * STRIDE] for t in range(5)], axis=0)


def with_modes(field, part):
    side = [part[8 * t : 8 * t + 8] for t in range(4)] + [jnp.zeros((8, LANES), f32)]
    return jnp.concatenate([field, jnp.concatenate(side, axis=1)], axis=0)


def modes_below(sent):
    tail = sent[COLS : COLS + 8]
    return jnp.concatenate([tail[:, t * STRIDE : (t + 1) * STRIDE] for t in range(4)], axis=0)


def pair_weights(own, far, w, xhi, xlo, j):
    w3 = jnp.concatenate(split3(w), axis=0)
    total = wide(jnp.sum(dot(w3, hot_twice(own), NT), axis=0, keepdims=True))
    total_far = wide(jnp.sum(dot(w3, hot_twice(far), NT), axis=0, keepdims=True))
    near = hot_paired(own)
    hi, mid, lo = split3(jnp.concatenate([w, w], axis=1))
    m = dot(jnp.concatenate([near * hi, near * mid, near * lo], axis=0), hot_paired(far), NT)
    m = m[0:LANES] + m[LANES : 2 * LANES] + m[2 * LANES :]
    hi, lo = split2(m)
    xhi[j] = hi
    xlo[j] = lo
    return total, total_far


def first_kernel(
    parity, b_in, k_in, q_in, nb_in, valid_in, left_in, right_in, penalty_in,
    blk1, blk0, band1, band0, tab, k,
    b, q, nb, valid, left, right, penalty, sem,
):
    small = [
        pltpu.make_async_copy(src, dst, sem.at[n])
        for n, (src, dst) in enumerate(
            [
                (nb_in, nb),
                (valid_in, valid),
                (left_in, left),
                (right_in, right),
                (penalty_in, penalty),
                (q_in, q),
                (b_in, b),
            ]
        )
    ]
    large = [
        pltpu.make_async_copy(
            k_in.at[a, :, pl.ds(m * LANES, LANES)], k.at[a, m], sem.at[8 + a * PAIRED + m]
        )
        for a in range(AGG)
        for m in range(PAIRED)
    ]
    for copy in small + large:
        copy.start()
    perm = permutation()
    expand = (iota((SLOTS, PAIRS), 0) == (iota((SLOTS, PAIRS), 1) >> 4)).astype(f32).astype(bf16)
    for copy in small:
        copy.wait()

    listed = jnp.concatenate([nb[...], valid[...]], axis=0).astype(f32).astype(bf16)
    listed = dot(listed, expand)
    slot = listed[0:AGG]
    weight = penalty[...] * listed[AGG:]
    crossing = slot > 3.5
    lf = left[...].astype(f32)
    rf = right[...].astype(f32)
    far = slot * 64.0 + rf
    wloc = jnp.where(crossing, 0.0, weight)
    wcross = jnp.where(crossing, weight, 0.0)
    tab[0:4] = lf
    tab[4:8] = rf
    tab[8:12] = far
    tab[12:16] = wloc
    tab[16:20] = wcross

    rr = iota((AGG * LANES, PAIRS), 0)
    row = (rr >> 7) * 64 + (rr & 63)
    lefts = lf.astype(jnp.int32)
    fars = far.astype(jnp.int32)
    hits = []
    for a in range(AGG):
        near = jnp.where(row == lefts[a : a + 1] + a * BLOCKS, 1.0, 0.0)
        hits.append((near + jnp.where(row == fars[a : a + 1], 1.0, 0.0)).astype(bf16))
    flat = jnp.concatenate([wloc[a : a + 1] for a in range(AGG)], axis=1)
    total = dot(jnp.concatenate(split3(flat), axis=0), jnp.concatenate(hits, axis=1), NT)
    total = jnp.sum(total, axis=0, keepdims=True)
    totals = []
    for a in range(AGG):
        tab[20 + a : 21 + a] = total[:, a * LANES : (a + 1) * LANES]
        totals.append(wide(total[:, a * LANES : (a + 1) * LANES]))

    pad = jnp.zeros((STRIDE - MODES, DOF), f32)
    q_all = q[...].astype(f32)
    modes = [jnp.concatenate([q_all[:, a, :], pad], axis=0).astype(bf16) for a in range(AGG)]
    turned_modes = dot(jnp.concatenate(modes, axis=0), perm)
    turned_modes = [turned_modes[a * STRIDE : (a + 1) * STRIDE] for a in range(AGG)]
    turned = mm_exact(jnp.concatenate([b[a] for a in range(AGG)], axis=0), perm)
    eye = iota((LANES, LANES), 0) == iota((LANES, LANES), 1)
    turned16 = [turned_modes[a].astype(bf16) for a in range(AGG)]
    springs = [mm2(turned_modes[a] * totals[a], turned16[a], NT) for a in range(AGG)]
    diagonals, wholes = [], []
    for copy in large:
        copy.wait()
    for a in range(AGG):
        cuts = []
        for m in range(PAIRED):
            tile = k[a, m, m * LANES : (m + 1) * LANES, :]
            cuts.append(jnp.sum(jnp.where(eye, tile, 0.0), axis=0, keepdims=True))
        diagonals.append(jnp.concatenate(cuts, axis=1))
        hi, lo = split2(jnp.concatenate([k[a, m] for m in range(PAIRED)], axis=1))
        projected = dot(modes[a], hi) + dot(modes[a], lo)
        wholes.append(mm2(projected, modes[a], NT) + springs[a])
    diagonals = mm_exact(jnp.concatenate(diagonals + [jnp.zeros((4, DOF), f32)], axis=0), perm)
    messages = []
    for a in range(AGG):
        load = turned[a * COLS : (a + 1) * COLS]
        diagonal = diagonals[a : a + 1] + totals[a]
        whole = wholes[a]
        table = jnp.concatenate([lf[a : a + 1], rf[a : a + 1], wcross[a : a + 1]], axis=1)
        side = [whole[8 * t : 8 * t + 8] for t in range(5)] + [jnp.zeros((8, STRIDE), f32)]
        messages.append(
            jnp.concatenate(
                [
                    load,
                    turned_modes[a][0:32],
                    jnp.concatenate([turned_modes[a][32:36], diagonal, table], axis=0),
                    jnp.zeros((2, DOF), f32),
                    jnp.concatenate(side, axis=1),
                ],
                axis=0,
            )
        )
    send(parity, messages, blk1, blk0, band1, band0)


def local_kernel(
    parity, blk1, blk0, band1, band0, tab, k,
    pkhi, pklo, ghi, glo, aqhi, aqlo, big, xhi, xlo, tco, tch, bp, qp, dsum, dloc, work,
):
    for a, sent in enumerate(receive(parity, blk1, blk0, band1, band0)):
        bp[a] = sent[0:COLS]
        qp[a] = sent_modes(sent)
        dsum[a] = sent_diagonal(sent)
        dloc[a : a + 1] = sent[68:69]
    perm = permutation()
    for a in range(AGG):
        tiles = []
        for m in range(PAIRED):
            picked = [k[a, m, pl.ds(c, BLOCKS, stride=6), :] for c in range(6)]
            tiles.append(jnp.concatenate(picked, axis=0))
        hi, lo = split2(jnp.concatenate(tiles, axis=1))
        both = dot(jnp.concatenate([hi, lo], axis=0), perm).astype(bf16)
        pkhi[a] = both[0:DOF]
        pklo[a] = both[DOF:]
    r = iota((AGG * LANES, 2 * PAIRS), 0)
    shift = 64 * (iota((1, 2 * PAIRS), 1) >> 7)
    rows = []
    for a in range(AGG):
        fi = tab[8 + a : 9 + a].astype(jnp.int32)
        fi = (fi >> 6) * LANES + (fi & 63)
        f2 = jnp.concatenate([fi] * 2, axis=1) + shift
        w2 = jnp.concatenate([tab[12 + a : 13 + a]] * 2, axis=1)
        far = (r == f2).astype(f32).astype(bf16)
        hi, mid, lo = split3(w2)
        near = hot_paired(tab[a : a + 1])
        parts = jnp.concatenate([near * hi, near * mid, near * lo], axis=0)
        m = dot(parts, far, NT)
        rows.append(m[0:LANES] + m[LANES : 2 * LANES] + m[2 * LANES :])
    mm = jnp.concatenate(rows, axis=0)
    work[...] = mm + mm.T
    eye = iota((AGG * LANES, AGG * LANES), 0) == iota((AGG * LANES, AGG * LANES), 1)
    total = jnp.concatenate([tab[20 + a : 21 + a] for a in range(AGG)], axis=1)
    gh, gl = split2(jnp.where(eye, total, 0.0) - work[...])
    ghi[...] = gh
    glo[...] = gl
    lines = []
    for a in range(AGG):
        rows = rows_of(qp[a].astype(f32)).astype(bf16)
        y = dot(rows, gh[a * LANES : (a + 1) * LANES]) + dot(rows, gl[a * LANES : (a + 1) * LANES])
        turned = dot(qp[a], pkhi[a]) + dot(qp[a], pklo[a])
        parts = []
        for c in range(AGG):
            part = lanes_of(y[:, c * LANES : (c + 1) * LANES])
            parts.append(part + turned if c == a else part)
        lines.append(jnp.concatenate(parts, axis=1))
    aq = jnp.concatenate(lines, axis=0)
    ah, al = split2(aq)
    aqhi[...] = ah
    aqlo[...] = al
    columns = []
    for a in range(AGG):
        both = jnp.concatenate([ah, al], axis=0)[:, a * DOF : (a + 1) * DOF]
        block = dot(both, qp[a], NT)
        columns.append(block[:WIDTH] + block[WIDTH:])
    big[...] = jnp.concatenate(columns, axis=1)
    for j in range(2, AGG):
        tco[j : j + 1], tch[j : j + 1] = pair_weights(
            tab[j : j + 1], tab[4 + j : 5 + j], tab[16 + j : 17 + j], xhi, xlo, j - 2
        )
    tco[0:2] = jnp.zeros((2, DOF), f32)
    tch[0:2] = jnp.zeros((2, DOF), f32)


def second_kernel(
    parity, blk1, blk0, band1, band0, bp, qp, dloc, khi, klo, ghi, glo, aqhi, aqlo, x2hi, x2lo, t2o, t2h,
    oblk1, oblk0, oband1, oband0, xhi, xlo, rec, rech, qh, cdh, tco, tch, x2o, r1o, dlt, pgo,
):
    halo = receive(parity, blk1, blk0, band1, band0)
    cross, xs, xh = [], [], []
    for j in range(AGG):
        if j < 2:
            table = halo[j][69:70]
            total, total_far = pair_weights(
                table[:, PAIRS : 2 * PAIRS], table[:, 0:PAIRS], table[:, 2 * PAIRS :], xhi, xlo, j
            )
        else:
            xhi[j] = x2hi[j - 2]
            xlo[j] = x2lo[j - 2]
            total, total_far = t2o[j : j + 1], t2h[j : j + 1]
        cross.append(total)
        tco[j : j + 1] = total
        tch[j : j + 1] = total_far
        inverse = fine_damping / (dloc[j : j + 1] + total)
        inverseh = fine_damping / (halo[j][68:69] + total_far)
        rec[j : j + 1] = inverse
        rech[j : j + 1] = inverseh
        qh[j] = sent_modes(halo[j])
        cdh[j] = sent_diagonal(halo[j])
        xs.append(inverse * bp[j])
        xh.append(inverseh * halo[j][0:COLS])
    kh = [khi[a] for a in range(AGG)]
    kl = [klo[a] for a in range(AGG)]
    y = local_product(xs, kh, kl, ghi[...], glo[...], cross)
    d, pg = [], []
    for j in range(AGG):
        r1 = bp[j] - y[j] + to_own(xh[j], xhi[j], xlo[j])
        step = rec[j : j + 1] * r1
        d.append(step)
        dlt[j] = step
        x2o[j] = xs[j] + step
        r1o[j] = r1
        pg.append(mm2(r1 - step * cross[j], qp[j], NT))
    pg = jnp.concatenate(pg, axis=1) - mm3(jnp.concatenate(d, axis=1), aqhi[...], aqlo[...], NT)
    pgo[...] = pg
    messages = []
    for j in range(AGG):
        part = pg[:, j * STRIDE : (j + 1) * STRIDE]
        messages.append(with_modes(d[j], part))
    send(parity, messages, oblk1, oblk0, oband1, oband0)


def inverse_kernel(
    pg, dlt, r1, khi, klo, ghi, glo, qp, qh, dsum, cdh, tco, tch, xhi, xlo, big,
    pr, yhi, ylo, zhi, zlo, vhi, vlo, q0, ghp, hhhi, hhlo, gchi, gclo, gxhi, gxlo, gohi, golo, work,
):
    d = [dlt[j] for j in range(AGG)]
    corner, couple, part = [], [], []
    for j in range(AGG):
        mine = qp[j].astype(f32)
        other = qh[j].astype(f32)
        own = mm2(mine * tco[j : j + 1], qp[j], NT)
        corner.append(own)
        blank = jnp.zeros((MODES, LANES - STRIDE), f32)
        work[:, j, :] = jnp.concatenate([dsum[j][0:MODES] + own[0:MODES], blank], axis=1)
        far = mm2(other * tch[j : j + 1], qh[j], NT)
        work[:, AGG + j, :] = jnp.concatenate([cdh[j][0:MODES] + far[0:MODES], blank], axis=1)

    def own_side(j):
        rows = rows_of(qp[j].astype(f32)).astype(bf16)
        y = lanes_of(dot(rows, xhi[j]) + dot(rows, xlo[j]))
        hi, lo = split2(y)
        yhi[j] = hi
        ylo[j] = lo
        couple.append(-(dot(hi, qh[j], NT) + dot(lo, qh[j], NT)))

    def far_side(j):
        rows = rows_of(qh[j].astype(f32)).astype(bf16)
        z = lanes_of(dot(rows, xhi[j], NT) + dot(rows, xlo[j], NT))
        hi, lo = split2(z)
        zhi[j] = hi
        zlo[j] = lo
        part.append(mm3(d[j], hi, lo, NT))

    springs = []

    def spring_side(j):
        if j == 0:
            springs.extend(unstack_fields(mm3(stack_fields(d), ghi[...], glo[...]), AGG))

    def bend_side(j):
        bend = mm3(d[j], khi[j], klo[j])
        pr[j] = r1[j] - (bend + (springs[j] + d[j] * tco[j : j + 1]))

    tasks = [(f, j) for f in (own_side, far_side, spring_side, bend_side) for j in range(AGG)]
    lane = iota((8, LANES), 1)
    rows = [work[i] + jnp.where(lane == STRIDE + i, 1.0, 0.0) for i in range(MODES)]

    def column(i, s):
        return jnp.broadcast_to(rows[i][:, s : s + 1], (8, LANES))

    for s in range(0, MODES, 2):
        p, q = s, s + 1
        pp, pq, qq, qp_ = column(p, p), column(p, q), column(q, q), column(q, p)
        scale = 1.0 / (pp * qq - pq * qp_)
        first = (qq * scale) * rows[p] - (pq * scale) * rows[q]
        second = (pp * scale) * rows[q] - (qp_ * scale) * rows[p]
        for i in range(MODES):
            if i != p and i != q:
                rows[i] = rows[i] - column(i, p) * first - column(i, q) * second
        rows[p], rows[q] = first, second
        if tasks:
            task, at = tasks.pop(0)
            task(at)
    for task, at in tasks:
        task(at)
    ghp[...] = jnp.concatenate(part, axis=1)
    for i in range(MODES):
        work[i] = rows[i] * coarse_damping
    below = jnp.zeros((STRIDE - MODES, STRIDE), f32)
    blocks = [
        jnp.concatenate([work[:, m, :][:, STRIDE:], below], axis=0) for m in range(2 * AGG)
    ]
    hh, hl = split2(block_diagonal(blocks[:AGG]))
    q0[...] = mm3(pg[...], hh, hl)
    for j in range(AGG):
        store2(vhi.at[j], vlo.at[j], mm3(blocks[j], yhi[j], ylo[j]))
    fh, fl = split2(block_diagonal(blocks[AGG:]))
    hhhi[...] = fh
    hhlo[...] = fl
    eye = iota((WIDTH, WIDTH), 0) == iota((WIDTH, WIDTH), 1)
    whole = big[...] + block_diagonal(corner)
    store2(gchi, gclo, jnp.where(eye, 1.0, 0.0) - mm3(whole, hh, hl))
    store2(gxhi, gxlo, -mm3(block_diagonal([c.T for c in couple]), hh, hl))
    store2(gohi, golo, -mm3(block_diagonal(couple), fh, fl))


def halo_modes(halo, at):
    return jnp.concatenate([h[:, at : at + STRIDE] for h in halo], axis=1)


def third_kernel(
    parity, blk1, blk0, band1, band0, q0, ghp, vhi, vlo, hhhi, hhlo, gchi, gclo, gxhi, gxlo,
    oblk1, oblk0, oband1, oband0, e1o, d1o, p2o, dh,
):
    halo = receive(parity, blk1, blk0, band1, band0)
    parts = []
    for j in range(AGG):
        value = halo[j][0:COLS]
        dh[j] = value
        parts.append(mm3(value, vhi[j], vlo[j], NT))
    e0 = q0[...] + jnp.concatenate(parts, axis=1)
    gh = jnp.concatenate([modes_below(h) for h in halo], axis=1) + ghp[...]
    e0h = mm3(gh, hhhi[...], hhlo[...])
    gch, gcl = gchi[...], gclo[...]
    d1 = mm3(e0, gch, gcl) + mm3(e0h, gxhi[...], gxlo[...])
    p2 = mm3(d1, gch, gcl)
    e1o[...] = e0 + d1
    d1o[...] = d1
    p2o[...] = p2
    messages = []
    for j in range(AGG):
        cut = slice(j * STRIDE, (j + 1) * STRIDE)
        messages.append(jnp.concatenate([d1[:, cut], p2[:, cut]], axis=1))
    send(parity, messages, oblk1, oblk0, oband1, oband0)


def beside_third_kernel(
    dh, pr, xhi, xlo, d1, e1, p2, gchi, gclo, gxhi, gxlo, gohi, golo, r2o, eo, gshi, gslo
):
    gch, gcl = gchi[...], gclo[...]
    gxh, gxl = gxhi[...], gxlo[...]
    gx = gxh.astype(f32) + gxl.astype(f32)
    store2(gshi, gslo, gx + mm3(gx, gch, gcl))
    w2 = mm3(d1[...], gohi[...], golo[...])
    eo[...] = e1[...] + p2[...] + mm3(p2[...], gch, gcl) + mm3(w2, gxh, gxl)
    for j in range(AGG):
        r2o[j] = pr[j] + to_own(dh[j], xhi[j], xlo[j])


def fourth_kernel(
    parity, blk1, blk0, band1, band0, ep, gshi, gslo, gxhi, gxlo, r2, qp, aqhi, aqlo, tco,
    oblk1, oblk0, oband1, oband0, eo, f3o, pr3o,
):
    halo = receive(parity, blk1, blk0, band1, band0)
    e = ep[...] + mm3(halo_modes(halo, 0), gshi[...], gslo[...])
    e = e + mm3(halo_modes(halo, STRIDE), gxhi[...], gxlo[...])
    eo[...] = e
    y = mm3(e, aqhi[...], aqlo[...])
    messages = []
    for j in range(AGG):
        mine = e[:, j * STRIDE : (j + 1) * STRIDE]
        f = mm2(mine, qp[j])
        f3o[j] = f
        part = r2[j] - y[:, j * DOF : (j + 1) * DOF] - f * tco[j : j + 1]
        pr3o[j] = part
        messages.append(with_modes(part, mine))
    send(parity, messages, oblk1, oblk0, oband1, oband0)


def beside_fourth_kernel(e, x2, f3, yhi, ylo, x3o, rho):
    for j in range(AGG):
        x3o[j] = x2[j] + f3[j]
        rho[j] = mm3(e[:, j * STRIDE : (j + 1) * STRIDE], yhi[j], ylo[j])


def last_kernel(
    parity, blk1, blk0, band1, band0, x3, pr3, rh3, zhi, zlo, rec, rech, khi, klo, ghi, glo, tco, xhi, xlo,
    field, residual,
):
    halo = receive(parity, blk1, blk0, band1, band0)
    d4, d4h, r3 = [], [], []
    for j in range(AGG):
        r = pr3[j] + mm3(modes_below(halo[j]), zhi[j], zlo[j])
        rh = halo[j][0:COLS] + rh3[j]
        r3.append(r)
        d4.append(rec[j : j + 1] * r)
        d4h.append(rech[j : j + 1] * rh)
    cross = [tco[j : j + 1] for j in range(AGG)]
    y = local_product(
        d4, [khi[a] for a in range(AGG)], [klo[a] for a in range(AGG)], ghi[...], glo[...], cross
    )
    out = []
    for j in range(AGG):
        out.append(x3[j] + d4[j])
    for j in range(AGG):
        out.append(r3[j] - y[j] + to_own(d4h[j], xhi[j], xlo[j]))
    turned = mm2(jnp.concatenate(out, axis=0), permutation_back())
    for j in range(AGG):
        field[j] = turned[j * COLS : (j + 1) * COLS]
        residual[j] = turned[(AGG + j) * COLS : (AGG + j + 1) * COLS]


VM = pl.BlockSpec(memory_space=pltpu.VMEM)
SM = pl.BlockSpec(memory_space=pltpu.SMEM)
HB = pl.BlockSpec(memory_space=pltpu.HBM)


def run(kernel, outs, *args, scalars=0, far=0, scratch=()):
    near = len(args) - far
    args = args[:near] + tuple(
        pltpu.with_memory_space_constraint(x, pltpu.HBM) for x in args[near:]
    )
    return pl.pallas_call(
        kernel,
        out_shape=[jax.ShapeDtypeStruct(shape, kind) for shape, kind in outs],
        in_specs=[SM] * scalars + [VM] * (near - scalars) + [HB] * far,
        out_specs=[VM] * len(outs),
        scratch_shapes=list(scratch),
        compiler_params=pltpu.CompilerParams(vmem_limit_bytes=24 * 2**20),
    )(*args)


def swapped(x, axis, odd):
    length = lax.axis_size(axis)
    route = []
    for i in range(odd, length + odd, 2):
        near, far = i % length, (i + 1) % length
        route += [(near, far), (far, near)]
    return lax.ppermute(x, axis, route)


def exchange(messages):
    blk1, blk0, band1, band0 = messages
    in0 = swapped(band0, "band", 0)
    in1 = swapped(band1, "band", 1)
    in2 = swapped(blk0, "blk", 0)
    in3 = swapped(blk1, "blk", 1)
    return in3, in2, in1, in0


def shards(
    load_columns, stiffness, rigid_modes, neighbours, slot_valid, pair_left, pair_right, penalty
):
    parity = jnp.stack([lax.axis_index("blk") % 2, lax.axis_index("band") % 2]).astype(jnp.int32)
    fields = ((AGG, COLS, DOF), f32)
    modes = ((AGG, STRIDE, DOF), bf16)
    square = ((AGG, DOF, DOF), bf16)
    local = ((AGG * LANES, AGG * LANES), bf16)
    small = ((AGG, 40, STRIDE), f32)
    tile = ((AGG, LANES, LANES), bf16)
    rows = ((AGG, DOF), f32)
    coarse = ((COLS, WIDTH), f32)
    broad = ((WIDTH, AGG * DOF), bf16)
    dense = ((WIDTH, WIDTH), bf16)

    def message(height, width):
        return [((height, width), f32)] * 4

    *out, tab, tiles = run(
        first_kernel,
        message(80, DOF) + [((24, PAIRS), f32), ((AGG, PAIRED, DOF, LANES), f32)],
        parity,
        load_columns[0, 0],
        stiffness[0, 0],
        jnp.transpose(rigid_modes[0, 0], (1, 0, 2)),
        neighbours[0, 0],
        slot_valid[0, 0],
        pair_left[0, 0],
        pair_right[0, 0],
        penalty[0, 0],
        scalars=1,
        far=8,
        scratch=[
            pltpu.VMEM((AGG, COLS, DOF), f32),
            pltpu.VMEM((MODES, AGG, DOF), bf16),
            pltpu.VMEM((AGG, SLOTS), jnp.int32),
            pltpu.VMEM((AGG, SLOTS), jnp.int32),
            pltpu.VMEM((AGG, PAIRS), jnp.int32),
            pltpu.VMEM((AGG, PAIRS), jnp.int32),
            pltpu.VMEM((AGG, PAIRS), f32),
            pltpu.SemaphoreType.DMA((8 + AGG * PAIRED,)),
        ],
    )
    got = exchange(out)
    pair_tile = ((2, LANES, LANES), bf16)
    pkhi, pklo, ghi, glo, aqhi, aqlo, big, x2hi, x2lo, t2o, t2h, bp, qp, dsum, dloc = run(
        local_kernel,
        [square, square, local, local, broad, broad, ((WIDTH, WIDTH), f32), pair_tile, pair_tile, rows, rows]
        + [fields, modes, small, rows],
        parity, *out, tab, tiles,
        scalars=1,
        scratch=[pltpu.VMEM((AGG * LANES, AGG * LANES), f32)],
    )
    *out, xhi, xlo, rec, rech, qh, cdh, tco, tch, x2, r1, dlt, pg = run(
        second_kernel,
        message(COLS + 8, DOF)
        + [tile, tile, rows, rows, modes, small, rows, rows, fields, fields, fields, coarse],
        parity, *got, bp, qp, dloc, pkhi, pklo, ghi, glo, aqhi, aqlo, x2hi, x2lo, t2o, t2h,
        scalars=1,
    )
    got = exchange(out)
    pr, yhi, ylo, zhi, zlo, vhi, vlo, q0, ghp, hhhi, hhlo, gchi, gclo, gxhi, gxlo, gohi, golo = run(
        inverse_kernel,
        [fields] + [modes] * 6 + [coarse, coarse] + [dense] * 8,
        pg, dlt, r1, pkhi, pklo, ghi, glo, qp, qh, dsum, cdh, tco, tch, xhi, xlo, big,
        scratch=[pltpu.VMEM((MODES, 2 * AGG, LANES), f32)],
    )
    *out, e1, d1, p2, dh = run(
        third_kernel,
        message(COLS, LANES) + [coarse, coarse, coarse, fields],
        parity, *got, q0, ghp, vhi, vlo, hhhi, hhlo, gchi, gclo, gxhi, gxlo,
        scalars=1,
    )
    got = exchange(out)
    r2, ep, gshi, gslo = run(
        beside_third_kernel,
        [fields, coarse, dense, dense],
        dh, pr, xhi, xlo, d1, e1, p2, gchi, gclo, gxhi, gxlo, gohi, golo,
    )
    *out, e, f3, pr3 = run(
        fourth_kernel,
        message(COLS + 8, DOF) + [coarse, fields, fields],
        parity, *got, ep, gshi, gslo, gxhi, gxlo, r2, qp, aqhi, aqlo, tco,
        scalars=1,
    )
    got = exchange(out)
    x3, rh3 = run(beside_fourth_kernel, [fields, fields], e, x2, f3, yhi, ylo)
    field, residual = run(
        last_kernel,
        [fields, fields],
        parity, *got, x3, pr3, rh3, zhi, zlo, rec, rech, pkhi, pklo, ghi, glo, tco, xhi, xlo,
        scalars=1,
    )
    return (field[None, None], residual[None, None])


def solution(mesh):
    in_specs = (
        P("band", "blk", None, None, None),
        P("band", "blk", None, None, None),
        P("band", "blk", None, None, None),
        P("band", "blk", None, None),
        P("band", "blk", None, None),
        P("band", "blk", None, None),
        P("band", "blk", None, None),
        P("band", "blk", None, None),
    )
    out_specs = (P("band", "blk", None, None, None), P("band", "blk", None, None, None))
    return jax.shard_map(shards, mesh=mesh, in_specs=in_specs, out_specs=out_specs, check_vma=False)
```

```python
import jax
import jax.numpy as jnp
from jax import lax
from jax.experimental import pallas as pl
from jax.experimental.pallas import tpu as pltpu
from jax.sharding import PartitionSpec as P

COLS = 32
BLOCKS = 64
DOF = 384
MODES = 36
SLOTS = 8
PAIRS = 128
AGG = 4
LANES = 128
PAIRED = 3
STRIDE = 64
WIDTH = AGG * STRIDE

fine_damping = 0.6
coarse_damping = 0.7
f32 = jnp.float32
bf16 = jnp.bfloat16

NN = (((1,), (0,)), ((), ()))
NT = (((1,), (1,)), ((), ()))


def dot(a, b, dims=NN):
    return lax.dot_general(a, b, dims, preferred_element_type=f32)


def split2(x):
    hi = x.astype(bf16)
    lo = (x - hi.astype(f32)).astype(bf16)
    return hi, lo


def split3(x):
    hi = x.astype(bf16)
    rest = x - hi.astype(f32)
    mid = rest.astype(bf16)
    lo = (rest - mid.astype(f32)).astype(bf16)
    return hi, mid, lo


def mm3(x, whi, wlo, dims=NN):
    rows = x.shape[0]
    hi, lo = split2(x)
    first = dot(jnp.concatenate([hi, lo], axis=0), whi, dims)
    return first[:rows] + first[rows:] + dot(hi, wlo, dims)


def mm2(x, w, dims=NN):
    rows = x.shape[0]
    hi, lo = split2(x)
    both = dot(jnp.concatenate([hi, lo], axis=0), w, dims)
    return both[:rows] + both[rows:]


def mm_exact(x, w, dims=NN):
    rows = x.shape[0]
    parts = dot(jnp.concatenate(split3(x), axis=0), w, dims)
    return parts[:rows] + parts[rows : 2 * rows] + parts[2 * rows :]


def iota(shape, axis):
    return lax.broadcasted_iota(jnp.int32, shape, axis)


def permutation():
    i = iota((DOF, DOF), 0)
    j = iota((DOF, DOF), 1)
    return (i == 6 * (j & 63) + (j >> 6)).astype(f32).astype(bf16)


def permutation_back():
    i = iota((DOF, DOF), 0)
    j = iota((DOF, DOF), 1)
    return (j == 6 * (i & 63) + (i >> 6)).astype(f32).astype(bf16)


def hot_twice(index):
    k = iota((LANES, PAIRS), 0) & 63
    return (k == index.astype(jnp.int32)).astype(f32).astype(bf16)


def hot_paired(index):
    r = iota((LANES, 2 * PAIRS), 0)
    doubled = jnp.concatenate([index.astype(jnp.int32)] * 2, axis=1)
    want = doubled + 64 * (iota((1, 2 * PAIRS), 1) >> 7)
    return (r == want).astype(f32).astype(bf16)


def wide(t):
    return jnp.concatenate([t] * PAIRED, axis=1)


def stack_fields(v):
    rows = []
    for m in range(PAIRED):
        rows.append(jnp.concatenate([x[:, m * LANES : (m + 1) * LANES] for x in v], axis=1))
    return jnp.concatenate(rows, axis=0)


def unstack_fields(y, count):
    out = []
    for a in range(count):
        parts = [
            y[m * COLS : (m + 1) * COLS, a * LANES : (a + 1) * LANES] for m in range(PAIRED)
        ]
        out.append(jnp.concatenate(parts, axis=1))
    return out


def rows_of(x):
    return jnp.concatenate([x[:, m * LANES : (m + 1) * LANES] for m in range(PAIRED)], axis=0)


def lanes_of(x):
    r = x.shape[0] // PAIRED
    return jnp.concatenate([x[m * r : (m + 1) * r] for m in range(PAIRED)], axis=1)


def local_product(v, khi, klo, ghi, glo, cross):
    springs = unstack_fields(mm3(stack_fields(v), ghi, glo), AGG)
    return [
        mm3(v[a], khi[a], klo[a]) + (springs[a] + v[a] * cross[a]) for a in range(AGG)
    ]


def to_own(vh, xhi, xlo):
    return lanes_of(mm3(rows_of(vh), xhi, xlo, NT))


def to_halo(v, xhi, xlo):
    return lanes_of(mm3(rows_of(v), xhi, xlo))


def pick(flag, a, b):
    return jnp.where(flag, a, b)


def send(parity, message, blk1, blk0, band1, band0):
    odd_s = parity[0] == 1
    odd_b = parity[1] == 1
    blk1[...] = pick(odd_s, message[2], message[0])
    blk0[...] = pick(odd_s, message[0], message[2])
    band1[...] = pick(odd_b, message[3], message[1])
    band0[...] = pick(odd_b, message[1], message[3])


def receive(parity, blk1, blk0, band1, band0):
    odd_s = parity[0] == 1
    odd_b = parity[1] == 1
    blk1, blk0, band1, band0 = blk1[...], blk0[...], band1[...], band0[...]
    return [
        pick(odd_s, blk0, blk1),
        pick(odd_b, band0, band1),
        pick(odd_s, blk1, blk0),
        pick(odd_b, band1, band0),
    ]


def block_diagonal(blocks):
    rows = []
    for j in range(AGG):
        parts = []
        if j > 0:
            parts.append(jnp.zeros((STRIDE, j * STRIDE), f32))
        parts.append(blocks[j])
        if j < AGG - 1:
            parts.append(jnp.zeros((STRIDE, (AGG - 1 - j) * STRIDE), f32))
        rows.append(jnp.concatenate(parts, axis=1))
    return jnp.concatenate(rows, axis=0)


def store2(hi_ref, lo_ref, x):
    hi, lo = split2(x)
    hi_ref[...] = hi
    lo_ref[...] = lo


def sent_modes(sent):
    pad = jnp.zeros((STRIDE - MODES, DOF), f32)
    return jnp.concatenate([sent[32:68], pad], axis=0).astype(bf16)


def sent_diagonal(sent):
    tail = sent[72:80]
    return jnp.concatenate([tail[:, t * STRIDE : (t + 1) * STRIDE] for t in range(5)], axis=0)


def with_modes(field, part):
    side = [part[8 * t : 8 * t + 8] for t in range(4)] + [jnp.zeros((8, LANES), f32)]
    return jnp.concatenate([field, jnp.concatenate(side, axis=1)], axis=0)


def modes_below(sent):
    tail = sent[COLS : COLS + 8]
    return jnp.concatenate([tail[:, t * STRIDE : (t + 1) * STRIDE] for t in range(4)], axis=0)


def pair_weights(own, far, w, xhi, xlo, j):
    w3 = jnp.concatenate(split3(w), axis=0)
    total = wide(jnp.sum(dot(w3, hot_twice(own), NT), axis=0, keepdims=True))
    total_far = wide(jnp.sum(dot(w3, hot_twice(far), NT), axis=0, keepdims=True))
    near = hot_paired(own)
    hi, mid, lo = split3(jnp.concatenate([w, w], axis=1))
    m = dot(jnp.concatenate([near * hi, near * mid, near * lo], axis=0), hot_paired(far), NT)
    m = m[0:LANES] + m[LANES : 2 * LANES] + m[2 * LANES :]
    hi, lo = split2(m)
    xhi[j] = hi
    xlo[j] = lo
    return total, total_far


def first_kernel(
    parity, b_in, k_in, q_in, nb_in, valid_in, left_in, right_in, penalty_in,
    blk1, blk0, band1, band0, tab, k,
    b, q, nb, valid, left, right, penalty, sem,
):
    small = [
        pltpu.make_async_copy(src, dst, sem.at[n])
        for n, (src, dst) in enumerate(
            [
                (nb_in, nb),
                (valid_in, valid),
                (left_in, left),
                (right_in, right),
                (penalty_in, penalty),
                (q_in, q),
                (b_in, b),
            ]
        )
    ]
    large = [
        pltpu.make_async_copy(
            k_in.at[a, :, pl.ds(m * LANES, LANES)], k.at[a, m], sem.at[8 + a * PAIRED + m]
        )
        for a in range(AGG)
        for m in range(PAIRED)
    ]
    for copy in small + large:
        copy.start()
    perm = permutation()
    expand = (iota((SLOTS, PAIRS), 0) == (iota((SLOTS, PAIRS), 1) >> 4)).astype(f32).astype(bf16)
    for copy in small:
        copy.wait()

    listed = jnp.concatenate([nb[...], valid[...]], axis=0).astype(f32).astype(bf16)
    listed = dot(listed, expand)
    slot = listed[0:AGG]
    weight = penalty[...] * listed[AGG:]
    crossing = slot > 3.5
    lf = left[...].astype(f32)
    rf = right[...].astype(f32)
    far = slot * 64.0 + rf
    wloc = jnp.where(crossing, 0.0, weight)
    wcross = jnp.where(crossing, weight, 0.0)
    tab[0:4] = lf
    tab[4:8] = rf
    tab[8:12] = far
    tab[12:16] = wloc
    tab[16:20] = wcross

    rr = iota((AGG * LANES, PAIRS), 0)
    row = (rr >> 7) * 64 + (rr & 63)
    lefts = lf.astype(jnp.int32)
    fars = far.astype(jnp.int32)
    hits = []
    for a in range(AGG):
        near = jnp.where(row == lefts[a : a + 1] + a * BLOCKS, 1.0, 0.0)
        hits.append((near + jnp.where(row == fars[a : a + 1], 1.0, 0.0)).astype(bf16))
    flat = jnp.concatenate([wloc[a : a + 1] for a in range(AGG)], axis=1)
    total = dot(jnp.concatenate(split3(flat), axis=0), jnp.concatenate(hits, axis=1), NT)
    total = jnp.sum(total, axis=0, keepdims=True)
    totals = []
    for a in range(AGG):
        tab[20 + a : 21 + a] = total[:, a * LANES : (a + 1) * LANES]
        totals.append(wide(total[:, a * LANES : (a + 1) * LANES]))

    pad = jnp.zeros((STRIDE - MODES, DOF), f32)
    q_all = q[...].astype(f32)
    modes = [jnp.concatenate([q_all[:, a, :], pad], axis=0).astype(bf16) for a in range(AGG)]
    turned_modes = dot(jnp.concatenate(modes, axis=0), perm)
    turned_modes = [turned_modes[a * STRIDE : (a + 1) * STRIDE] for a in range(AGG)]
    turned = mm_exact(jnp.concatenate([b[a] for a in range(AGG)], axis=0), perm)
    eye = iota((LANES, LANES), 0) == iota((LANES, LANES), 1)
    turned16 = [turned_modes[a].astype(bf16) for a in range(AGG)]
    springs = [mm2(turned_modes[a] * totals[a], turned16[a], NT) for a in range(AGG)]
    diagonals, wholes = [], []
    for copy in large:
        copy.wait()
    for a in range(AGG):
        cuts = []
        for m in range(PAIRED):
            tile = k[a, m, m * LANES : (m + 1) * LANES, :]
            cuts.append(jnp.sum(jnp.where(eye, tile, 0.0), axis=0, keepdims=True))
        diagonals.append(jnp.concatenate(cuts, axis=1))
        hi, lo = split2(jnp.concatenate([k[a, m] for m in range(PAIRED)], axis=1))
        projected = dot(modes[a], hi) + dot(modes[a], lo)
        wholes.append(mm2(projected, modes[a], NT) + springs[a])
    diagonals = mm_exact(jnp.concatenate(diagonals + [jnp.zeros((4, DOF), f32)], axis=0), perm)
    messages = []
    for a in range(AGG):
        load = turned[a * COLS : (a + 1) * COLS]
        diagonal = diagonals[a : a + 1] + totals[a]
        whole = wholes[a]
        table = jnp.concatenate([lf[a : a + 1], rf[a : a + 1], wcross[a : a + 1]], axis=1)
        side = [whole[8 * t : 8 * t + 8] for t in range(5)] + [jnp.zeros((8, STRIDE), f32)]
        messages.append(
            jnp.concatenate(
                [
                    load,
                    turned_modes[a][0:32],
                    jnp.concatenate([turned_modes[a][32:36], diagonal, table], axis=0),
                    jnp.zeros((2, DOF), f32),
                    jnp.concatenate(side, axis=1),
                ],
                axis=0,
            )
        )
    send(parity, messages, blk1, blk0, band1, band0)


def local_kernel(
    parity, blk1, blk0, band1, band0, tab, k,
    pkhi, pklo, ghi, glo, aqhi, aqlo, big, xhi, xlo, tco, tch, bp, qp, dsum, dloc, early, work,
):
    for a, sent in enumerate(receive(parity, blk1, blk0, band1, band0)):
        bp[a] = sent[0:COLS]
        qp[a] = sent_modes(sent)
        dsum[a] = sent_diagonal(sent)
        dloc[a : a + 1] = sent[68:69]
    perm = permutation()
    for a in range(AGG):
        tiles = []
        for m in range(PAIRED):
            picked = [k[a, m, pl.ds(c, BLOCKS, stride=6), :] for c in range(6)]
            tiles.append(jnp.concatenate(picked, axis=0))
        hi, lo = split2(jnp.concatenate(tiles, axis=1))
        both = dot(jnp.concatenate([hi, lo], axis=0), perm).astype(bf16)
        pkhi[a] = both[0:DOF]
        pklo[a] = both[DOF:]
    r = iota((AGG * LANES, 2 * PAIRS), 0)
    shift = 64 * (iota((1, 2 * PAIRS), 1) >> 7)
    rows = []
    for a in range(AGG):
        fi = tab[8 + a : 9 + a].astype(jnp.int32)
        fi = (fi >> 6) * LANES + (fi & 63)
        f2 = jnp.concatenate([fi] * 2, axis=1) + shift
        w2 = jnp.concatenate([tab[12 + a : 13 + a]] * 2, axis=1)
        far = (r == f2).astype(f32).astype(bf16)
        hi, mid, lo = split3(w2)
        near = hot_paired(tab[a : a + 1])
        parts = jnp.concatenate([near * hi, near * mid, near * lo], axis=0)
        m = dot(parts, far, NT)
        rows.append(m[0:LANES] + m[LANES : 2 * LANES] + m[2 * LANES :])
    mm = jnp.concatenate(rows, axis=0)
    work[...] = mm + mm.T
    eye = iota((AGG * LANES, AGG * LANES), 0) == iota((AGG * LANES, AGG * LANES), 1)
    total = jnp.concatenate([tab[20 + a : 21 + a] for a in range(AGG)], axis=1)
    gh, gl = split2(jnp.where(eye, total, 0.0) - work[...])
    ghi[...] = gh
    glo[...] = gl
    lines = []
    for a in range(AGG):
        rows = rows_of(qp[a].astype(f32)).astype(bf16)
        y = dot(rows, gh[a * LANES : (a + 1) * LANES]) + dot(rows, gl[a * LANES : (a + 1) * LANES])
        turned = dot(qp[a], pkhi[a]) + dot(qp[a], pklo[a])
        parts = []
        for c in range(AGG):
            part = lanes_of(y[:, c * LANES : (c + 1) * LANES])
            parts.append(part + turned if c == a else part)
        lines.append(jnp.concatenate(parts, axis=1))
    aq = jnp.concatenate(lines, axis=0)
    ah, al = split2(aq)
    aqhi[...] = ah
    aqlo[...] = al
    columns = []
    for a in range(AGG):
        both = jnp.concatenate([ah, al], axis=0)[:, a * DOF : (a + 1) * DOF]
        block = dot(both, qp[a], NT)
        columns.append(block[:WIDTH] + block[WIDTH:])
    big[...] = jnp.concatenate(columns, axis=1)
    for j in range(2, AGG):
        tco[j : j + 1], tch[j : j + 1] = pair_weights(
            tab[j : j + 1], tab[4 + j : 5 + j], tab[16 + j : 17 + j], xhi, xlo, j - 2
        )
    for j in range(2, AGG):
        x = fine_damping / (dloc[j : j + 1] + tco[j : j + 1]) * bp[j]
        early[j - 2] = mm3(x, pkhi[j], pklo[j])
    tco[0:2] = jnp.zeros((2, DOF), f32)
    tch[0:2] = jnp.zeros((2, DOF), f32)


def second_kernel(
    parity, blk1, blk0, band1, band0, bp, qp, dloc, khi, klo, ghi, glo, aqhi, aqlo, x2hi, x2lo, t2o, t2h, early,
    oblk1, oblk0, oband1, oband0, xhi, xlo, rec, rech, qh, cdh, tco, tch, x2o, r1o, dlt, pgo,
):
    halo = receive(parity, blk1, blk0, band1, band0)
    cross, xs, xh = [], [], []
    for j in range(AGG):
        if j < 2:
            table = halo[j][69:70]
            total, total_far = pair_weights(
                table[:, PAIRS : 2 * PAIRS], table[:, 0:PAIRS], table[:, 2 * PAIRS :], xhi, xlo, j
            )
        else:
            xhi[j] = x2hi[j - 2]
            xlo[j] = x2lo[j - 2]
            total, total_far = t2o[j : j + 1], t2h[j : j + 1]
        cross.append(total)
        tco[j : j + 1] = total
        tch[j : j + 1] = total_far
        inverse = fine_damping / (dloc[j : j + 1] + total)
        inverseh = fine_damping / (halo[j][68:69] + total_far)
        rec[j : j + 1] = inverse
        rech[j : j + 1] = inverseh
        qh[j] = sent_modes(halo[j])
        cdh[j] = sent_diagonal(halo[j])
        xs.append(inverse * bp[j])
        xh.append(inverseh * halo[j][0:COLS])
    springs = unstack_fields(mm3(stack_fields(xs), ghi[...], glo[...]), AGG)
    y = []
    for a in range(AGG):
        bend = mm3(xs[a], khi[a], klo[a]) if a < 2 else early[a - 2]
        y.append(bend + (springs[a] + xs[a] * cross[a]))
    d, pg = [], []
    for j in range(AGG):
        r1 = bp[j] - y[j] + to_own(xh[j], xhi[j], xlo[j])
        step = rec[j : j + 1] * r1
        d.append(step)
        dlt[j] = step
        x2o[j] = xs[j] + step
        r1o[j] = r1
        pg.append(mm2(r1 - step * cross[j], qp[j], NT))
    pg = jnp.concatenate(pg, axis=1) - mm3(jnp.concatenate(d, axis=1), aqhi[...], aqlo[...], NT)
    pgo[...] = pg
    messages = []
    for j in range(AGG):
        part = pg[:, j * STRIDE : (j + 1) * STRIDE]
        messages.append(with_modes(d[j], part))
    send(parity, messages, oblk1, oblk0, oband1, oband0)


def inverse_kernel(
    pg, dlt, r1, khi, klo, ghi, glo, qp, qh, dsum, cdh, tco, tch, xhi, xlo, big,
    pr, yhi, ylo, zhi, zlo, vhi, vlo, q0, ghp, hhhi, hhlo, gchi, gclo, gxhi, gxlo, gohi, golo, work,
):
    d = [dlt[j] for j in range(AGG)]
    corner, couple, part = [], [], []
    for j in range(AGG):
        mine = qp[j].astype(f32)
        other = qh[j].astype(f32)
        own = mm2(mine * tco[j : j + 1], qp[j], NT)
        corner.append(own)
        blank = jnp.zeros((MODES, LANES - STRIDE), f32)
        work[:, j, :] = jnp.concatenate([dsum[j][0:MODES] + own[0:MODES], blank], axis=1)
        far = mm2(other * tch[j : j + 1], qh[j], NT)
        work[:, AGG + j, :] = jnp.concatenate([cdh[j][0:MODES] + far[0:MODES], blank], axis=1)

    def own_side(j):
        rows = rows_of(qp[j].astype(f32)).astype(bf16)
        y = lanes_of(dot(rows, xhi[j]) + dot(rows, xlo[j]))
        hi, lo = split2(y)
        yhi[j] = hi
        ylo[j] = lo
        couple.append(-(dot(hi, qh[j], NT) + dot(lo, qh[j], NT)))

    def far_side(j):
        rows = rows_of(qh[j].astype(f32)).astype(bf16)
        z = lanes_of(dot(rows, xhi[j], NT) + dot(rows, xlo[j], NT))
        hi, lo = split2(z)
        zhi[j] = hi
        zlo[j] = lo
        part.append(mm3(d[j], hi, lo, NT))

    springs = []

    def spring_side(j):
        if j == 0:
            springs.extend(unstack_fields(mm3(stack_fields(d), ghi[...], glo[...]), AGG))

    def bend_side(j):
        bend = mm3(d[j], khi[j], klo[j])
        pr[j] = r1[j] - (bend + (springs[j] + d[j] * tco[j : j + 1]))

    tasks = [(f, j) for f in (own_side, far_side, spring_side, bend_side) for j in range(AGG)]
    lane = iota((8, LANES), 1)
    rows = [work[i] + jnp.where(lane == STRIDE + i, 1.0, 0.0) for i in range(MODES)]

    def column(i, s):
        return jnp.broadcast_to(rows[i][:, s : s + 1], (8, LANES))

    for s in range(0, MODES, 2):
        p, q = s, s + 1
        pp, pq, qq, qp_ = column(p, p), column(p, q), column(q, q), column(q, p)
        scale = 1.0 / (pp * qq - pq * qp_)
        first = (qq * scale) * rows[p] - (pq * scale) * rows[q]
        second = (pp * scale) * rows[q] - (qp_ * scale) * rows[p]
        for i in range(MODES):
            if i != p and i != q:
                rows[i] = rows[i] - column(i, p) * first - column(i, q) * second
        rows[p], rows[q] = first, second
        if tasks:
            task, at = tasks.pop(0)
            task(at)
    for task, at in tasks:
        task(at)
    ghp[...] = jnp.concatenate(part, axis=1)
    for i in range(MODES):
        work[i] = rows[i] * coarse_damping
    below = jnp.zeros((STRIDE - MODES, STRIDE), f32)
    blocks = [
        jnp.concatenate([work[:, m, :][:, STRIDE:], below], axis=0) for m in range(2 * AGG)
    ]
    hh, hl = split2(block_diagonal(blocks[:AGG]))
    q0[...] = mm3(pg[...], hh, hl)
    for j in range(AGG):
        store2(vhi.at[j], vlo.at[j], mm3(blocks[j], yhi[j], ylo[j]))
    fh, fl = split2(block_diagonal(blocks[AGG:]))
    hhhi[...] = fh
    hhlo[...] = fl
    eye = iota((WIDTH, WIDTH), 0) == iota((WIDTH, WIDTH), 1)
    whole = big[...] + block_diagonal(corner)
    store2(gchi, gclo, jnp.where(eye, 1.0, 0.0) - mm3(whole, hh, hl))
    store2(gxhi, gxlo, -mm3(block_diagonal([c.T for c in couple]), hh, hl))
    store2(gohi, golo, -mm3(block_diagonal(couple), fh, fl))


def halo_modes(halo, at):
    return jnp.concatenate([h[:, at : at + STRIDE] for h in halo], axis=1)


def third_kernel(
    parity, blk1, blk0, band1, band0, q0, ghp, vhi, vlo, hhhi, hhlo, gchi, gclo, gxhi, gxlo,
    oblk1, oblk0, oband1, oband0, e1o, d1o, p2o, dh,
):
    halo = receive(parity, blk1, blk0, band1, band0)
    parts = []
    for j in range(AGG):
        value = halo[j][0:COLS]
        dh[j] = value
        parts.append(mm3(value, vhi[j], vlo[j], NT))
    e0 = q0[...] + jnp.concatenate(parts, axis=1)
    gh = jnp.concatenate([modes_below(h) for h in halo], axis=1) + ghp[...]
    e0h = mm3(gh, hhhi[...], hhlo[...])
    gch, gcl = gchi[...], gclo[...]
    d1 = mm3(e0, gch, gcl) + mm3(e0h, gxhi[...], gxlo[...])
    p2 = mm3(d1, gch, gcl)
    e1o[...] = e0 + d1
    d1o[...] = d1
    p2o[...] = p2
    messages = []
    for j in range(AGG):
        cut = slice(j * STRIDE, (j + 1) * STRIDE)
        messages.append(jnp.concatenate([d1[:, cut], p2[:, cut]], axis=1))
    send(parity, messages, oblk1, oblk0, oband1, oband0)


def beside_third_kernel(
    dh, pr, xhi, xlo, d1, e1, p2, gchi, gclo, gxhi, gxlo, gohi, golo, r2o, eo, gshi, gslo
):
    gch, gcl = gchi[...], gclo[...]
    gxh, gxl = gxhi[...], gxlo[...]
    gx = gxh.astype(f32) + gxl.astype(f32)
    store2(gshi, gslo, gx + mm3(gx, gch, gcl))
    w2 = mm3(d1[...], gohi[...], golo[...])
    eo[...] = e1[...] + p2[...] + mm3(p2[...], gch, gcl) + mm3(w2, gxh, gxl)
    for j in range(AGG):
        r2o[j] = pr[j] + to_own(dh[j], xhi[j], xlo[j])


def fourth_kernel(
    parity, blk1, blk0, band1, band0, ep, gshi, gslo, gxhi, gxlo, r2, qp, aqhi, aqlo, tco,
    oblk1, oblk0, oband1, oband0, eo, f3o, pr3o,
):
    halo = receive(parity, blk1, blk0, band1, band0)
    e = ep[...] + mm3(halo_modes(halo, 0), gshi[...], gslo[...])
    e = e + mm3(halo_modes(halo, STRIDE), gxhi[...], gxlo[...])
    eo[...] = e
    y = mm3(e, aqhi[...], aqlo[...])
    messages = []
    for j in range(AGG):
        mine = e[:, j * STRIDE : (j + 1) * STRIDE]
        f = mm2(mine, qp[j])
        f3o[j] = f
        part = r2[j] - y[:, j * DOF : (j + 1) * DOF] - f * tco[j : j + 1]
        pr3o[j] = part
        messages.append(with_modes(part, mine))
    send(parity, messages, oblk1, oblk0, oband1, oband0)


def beside_fourth_kernel(e, x2, f3, yhi, ylo, x3o, rho):
    for j in range(AGG):
        x3o[j] = x2[j] + f3[j]
        rho[j] = mm3(e[:, j * STRIDE : (j + 1) * STRIDE], yhi[j], ylo[j])


def last_kernel(
    parity, blk1, blk0, band1, band0, x3, pr3, rh3, zhi, zlo, rec, rech, khi, klo, ghi, glo, tco, xhi, xlo,
    field, residual,
):
    halo = receive(parity, blk1, blk0, band1, band0)
    d4, d4h, r3 = [], [], []
    for j in range(AGG):
        r = pr3[j] + mm3(modes_below(halo[j]), zhi[j], zlo[j])
        rh = halo[j][0:COLS] + rh3[j]
        r3.append(r)
        d4.append(rec[j : j + 1] * r)
        d4h.append(rech[j : j + 1] * rh)
    cross = [tco[j : j + 1] for j in range(AGG)]
    y = local_product(
        d4, [khi[a] for a in range(AGG)], [klo[a] for a in range(AGG)], ghi[...], glo[...], cross
    )
    out = []
    for j in range(AGG):
        out.append(x3[j] + d4[j])
    for j in range(AGG):
        out.append(r3[j] - y[j] + to_own(d4h[j], xhi[j], xlo[j]))
    turned = mm2(jnp.concatenate(out, axis=0), permutation_back())
    for j in range(AGG):
        field[j] = turned[j * COLS : (j + 1) * COLS]
        residual[j] = turned[(AGG + j) * COLS : (AGG + j + 1) * COLS]


VM = pl.BlockSpec(memory_space=pltpu.VMEM)
SM = pl.BlockSpec(memory_space=pltpu.SMEM)
HB = pl.BlockSpec(memory_space=pltpu.HBM)


def run(kernel, outs, *args, scalars=0, far=0, scratch=()):
    near = len(args) - far
    args = args[:near] + tuple(
        pltpu.with_memory_space_constraint(x, pltpu.HBM) for x in args[near:]
    )
    return pl.pallas_call(
        kernel,
        out_shape=[jax.ShapeDtypeStruct(shape, kind) for shape, kind in outs],
        in_specs=[SM] * scalars + [VM] * (near - scalars) + [HB] * far,
        out_specs=[VM] * len(outs),
        scratch_shapes=list(scratch),
        compiler_params=pltpu.CompilerParams(vmem_limit_bytes=24 * 2**20),
    )(*args)


def swapped(x, axis, odd):
    length = lax.axis_size(axis)
    route = []
    for i in range(odd, length + odd, 2):
        near, far = i % length, (i + 1) % length
        route += [(near, far), (far, near)]
    return lax.ppermute(x, axis, route)


def exchange(messages):
    blk1, blk0, band1, band0 = messages
    in0 = swapped(band0, "band", 0)
    in1 = swapped(band1, "band", 1)
    in2 = swapped(blk0, "blk", 0)
    in3 = swapped(blk1, "blk", 1)
    return in3, in2, in1, in0


def shards(
    load_columns, stiffness, rigid_modes, neighbours, slot_valid, pair_left, pair_right, penalty
):
    parity = jnp.stack([lax.axis_index("blk") % 2, lax.axis_index("band") % 2]).astype(jnp.int32)
    fields = ((AGG, COLS, DOF), f32)
    modes = ((AGG, STRIDE, DOF), bf16)
    square = ((AGG, DOF, DOF), bf16)
    local = ((AGG * LANES, AGG * LANES), bf16)
    small = ((AGG, 40, STRIDE), f32)
    tile = ((AGG, LANES, LANES), bf16)
    rows = ((AGG, DOF), f32)
    coarse = ((COLS, WIDTH), f32)
    broad = ((WIDTH, AGG * DOF), bf16)
    dense = ((WIDTH, WIDTH), bf16)

    def message(height, width):
        return [((height, width), f32)] * 4

    *out, tab, tiles = run(
        first_kernel,
        message(80, DOF) + [((24, PAIRS), f32), ((AGG, PAIRED, DOF, LANES), f32)],
        parity,
        load_columns[0, 0],
        stiffness[0, 0],
        jnp.transpose(rigid_modes[0, 0], (1, 0, 2)),
        neighbours[0, 0],
        slot_valid[0, 0],
        pair_left[0, 0],
        pair_right[0, 0],
        penalty[0, 0],
        scalars=1,
        far=8,
        scratch=[
            pltpu.VMEM((AGG, COLS, DOF), f32),
            pltpu.VMEM((MODES, AGG, DOF), bf16),
            pltpu.VMEM((AGG, SLOTS), jnp.int32),
            pltpu.VMEM((AGG, SLOTS), jnp.int32),
            pltpu.VMEM((AGG, PAIRS), jnp.int32),
            pltpu.VMEM((AGG, PAIRS), jnp.int32),
            pltpu.VMEM((AGG, PAIRS), f32),
            pltpu.SemaphoreType.DMA((8 + AGG * PAIRED,)),
        ],
    )
    got = exchange(out)
    pair_tile = ((2, LANES, LANES), bf16)
    pkhi, pklo, ghi, glo, aqhi, aqlo, big, x2hi, x2lo, t2o, t2h, bp, qp, dsum, dloc, early = run(
        local_kernel,
        [square, square, local, local, broad, broad, ((WIDTH, WIDTH), f32), pair_tile, pair_tile, rows, rows]
        + [fields, modes, small, rows, ((2, COLS, DOF), f32)],
        parity, *out, tab, tiles,
        scalars=1,
        scratch=[pltpu.VMEM((AGG * LANES, AGG * LANES), f32)],
    )
    *out, xhi, xlo, rec, rech, qh, cdh, tco, tch, x2, r1, dlt, pg = run(
        second_kernel,
        message(COLS + 8, DOF)
        + [tile, tile, rows, rows, modes, small, rows, rows, fields, fields, fields, coarse],
        parity, *got, bp, qp, dloc, pkhi, pklo, ghi, glo, aqhi, aqlo, x2hi, x2lo, t2o, t2h, early,
        scalars=1,
    )
    got = exchange(out)
    pr, yhi, ylo, zhi, zlo, vhi, vlo, q0, ghp, hhhi, hhlo, gchi, gclo, gxhi, gxlo, gohi, golo = run(
        inverse_kernel,
        [fields] + [modes] * 6 + [coarse, coarse] + [dense] * 8,
        pg, dlt, r1, pkhi, pklo, ghi, glo, qp, qh, dsum, cdh, tco, tch, xhi, xlo, big,
        scratch=[pltpu.VMEM((MODES, 2 * AGG, LANES), f32)],
    )
    *out, e1, d1, p2, dh = run(
        third_kernel,
        message(COLS, LANES) + [coarse, coarse, coarse, fields],
        parity, *got, q0, ghp, vhi, vlo, hhhi, hhlo, gchi, gclo, gxhi, gxlo,
        scalars=1,
    )
    got = exchange(out)
    r2, ep, gshi, gslo = run(
        beside_third_kernel,
        [fields, coarse, dense, dense],
        dh, pr, xhi, xlo, d1, e1, p2, gchi, gclo, gxhi, gxlo, gohi, golo,
    )
    *out, e, f3, pr3 = run(
        fourth_kernel,
        message(COLS + 8, DOF) + [coarse, fields, fields],
        parity, *got, ep, gshi, gslo, gxhi, gxlo, r2, qp, aqhi, aqlo, tco,
        scalars=1,
    )
    got = exchange(out)
    x3, rh3 = run(beside_fourth_kernel, [fields, fields], e, x2, f3, yhi, ylo)
    field, residual = run(
        last_kernel,
        [fields, fields],
        parity, *got, x3, pr3, rh3, zhi, zlo, rec, rech, pkhi, pklo, ghi, glo, tco, xhi, xlo,
        scalars=1,
    )
    return (field[None, None], residual[None, None])


def solution(mesh):
    in_specs = (
        P("band", "blk", None, None, None),
        P("band", "blk", None, None, None),
        P("band", "blk", None, None, None),
        P("band", "blk", None, None),
        P("band", "blk", None, None),
        P("band", "blk", None, None),
        P("band", "blk", None, None),
        P("band", "blk", None, None),
    )
    out_specs = (P("band", "blk", None, None, None), P("band", "blk", None, None, None))
    return jax.shard_map(shards, mesh=mesh, in_specs=in_specs, out_specs=out_specs, check_vma=False)
```
